32 devices in a mesh: seg: 4 (over y, x), rank: 8 (over z, core).
Axes of the slice: x: 2, y: 2, z: 4, core: 2. Of those that a mesh axis runs over, the one named last changes fastest.
Arguments:
- parent_nodes: float32 [81920, 375], P(('seg', 'rank')), as said below
- marks: int32 [32, 256], P(('seg', 'rank')), may hold values from 0 to 2559, as said below
- child_owner: int32 [65536, 1], P(('seg', 'rank')), may hold values from 0 to 31; in each aligned block of 2048 rows (0 to 2047, 2048 to 4095, ...) at most 128 rows name the same one
- face_link: int32 [131072, 6], P(('seg', 'rank')), may hold values from 0 to 12287
Outputs:
- node_mass: float32 [125, 131072], P(None, ('seg', 'rank'))
- face_mass: float32 [150, 131072], P(None, ('seg', 'rank'))
The draws below stay inside these ranges and needn't reach their ends.
Inputs may be any that keep to these rules, and one draw needn't show every extreme that they name: `marks`: each row holds distinct local parent indices of its device. `child_owner`: among the children of one device no owner is named more than 128 times, a bound that some block reaches. `face_link`: the first 4096 values name slots of the previous owner along rank, the next 4096 own slots, the last 4096 slots of the next owner. `parent_nodes`: nodes of a slightly perturbed cube of side 3 to 6 around a point of the box from -8 to 8.
All inputs are finite; a program needn't handle non-finite values.
Results may differ from the reference program's by a relative error of at most 0.0003.
Values sent between devices are 32-bit elements; how exact they have to be, the bound alone decides.
A program may use at most 192 MiB of HBM per device.

```python
import math
import jax
import jax.numpy as jnp
import numpy as np
from jax import lax

ELEM_DEV = 2560
MARKED = 256
KIDS = 2048
CAP = 128
SLOTS = 4096
ELEMS = 81920
KIDS_ALL = 65536
SLOTS_ALL = 131072
N_SEG = 4
N_RANK = 8


def draw_parent_nodes(key, part):
    points = np.array([-1.0, -math.sqrt(3.0 / 7.0), 0.0, math.sqrt(3.0 / 7.0), 1.0])
    lattice = np.zeros((3, 125))
    for i in range(5):
        for j in range(5):
            for k in range(5):
                lattice[0, i * 25 + j * 5 + k] = points[i]
                lattice[1, i * 25 + j * 5 + k] = points[j]
                lattice[2, i * 25 + j * 5 + k] = points[k]
    first_key, second_key, third_key = jax.random.split(key, 3)
    centre = jax.random.uniform(first_key, (ELEMS, 3, 1), jnp.float32, -8.0, 8.0)
    side = jnp.exp(jax.random.uniform(second_key, (ELEMS, 1, 1), jnp.float32, math.log(3.0), math.log(6.0)))
    jitter = 0.03 * jax.random.normal(third_key, (ELEMS, 3, 125), jnp.float32)
    nodes = centre + side * (0.5 * jnp.asarray(lattice, jnp.float32)[None] + jitter)
    return nodes.reshape(ELEMS, 375).astype(jnp.float32)


def draw_marks(key, part):
    devices = ELEMS // ELEM_DEV
    keys = jax.random.split(jax.random.fold_in(key, 17), devices)
    chosen = jax.vmap(lambda k: jax.random.permutation(k, ELEM_DEV)[:MARKED])(keys)
    return chosen.astype(jnp.int32)


def set_ends(values, own_key, smallest, high):
    shape = values.shape
    place = [jax.random.randint(jax.random.fold_in(own_key, axis), (), 0, shape[axis]) for axis in range(len(shape))]
    values = values.at[tuple(place)].set(smallest)
    longest = shape.index(max(shape))
    place[longest] = (place[longest] + 1) % shape[longest]
    return values.at[tuple(place)].set(high)


def routed_block(rng, own, number, rows, count, top, limit, skew):
    order = jax.random.permutation(rng, count)
    heavy_load, usual = portions_of(count, rows * top, limit, skew, True), portions_of(count, rows * top, limit, skew, False)
    places = jnp.arange(count)

    def named(sizes, rotation):
        used = int((sizes > 0).sum())
        fixed = max(1, used // 4)
        shifted = fixed + (places - fixed + rotation * (used - fixed)) % max(1, count - fixed)
        return jnp.zeros((count,), jnp.int32).at[order[jnp.where(places < fixed, places, shifted)]].set(jnp.asarray(sizes, jnp.int32))

    sizes = jnp.where(number % 4 == 0, named(heavy_load, number // 4), named(usual, number - number // 4 - 1))
    mixed = jax.random.permutation(jax.random.fold_in(own, 3), count)
    donor, receiver = mixed[0:count // 2 * 2:2], mixed[1:count // 2 * 2:2]
    room = jnp.minimum(sizes[donor] - 1, limit - sizes[receiver]) // 2
    room = jnp.where((donor == order[0]) | (receiver == order[0]) | (sizes[receiver] == 0), 0, jnp.maximum(room, 0))
    shifted = jax.random.randint(jax.random.fold_in(own, 4), (count // 2,), 0, 1 << 20) % (room + 1)
    sizes = sizes.at[donor].add(-shifted).at[receiver].add(shifted)
    labels = jnp.searchsorted(jnp.cumsum(sizes), jnp.arange(rows * top), side="right").astype(jnp.int32)
    table = labels.reshape(top, rows).T
    table = table[jax.random.permutation(jax.random.fold_in(own, 1), rows)]
    rotation = jax.random.randint(jax.random.fold_in(own, 2), (rows, 1), 0, top)
    return jnp.take_along_axis(table, (jnp.arange(top)[None, :] + rotation) % top, axis=1)


def portions_of(count, total, bound, slope, full):
    weights = [(1 << 20) // math.isqrt(grade ** slope) + 1 for grade in range(1, count + 1)]
    largest = bound if full else min(bound, max(-(-total // count), total * weights[0] // sum(weights)))
    least = 1 if total - largest >= count - 1 else 0
    holding, rest = [largest] + [least] * (count - 1), total - largest - least * (count - 1)
    while rest > 0:
        candidates = [i for i in range(1, count) if holding[i] < largest] or [i for i in range(1, count) if holding[i] < bound]
        whole, left = sum([weights[i] for i in candidates]), rest
        for i in candidates:
            addition = min(bound - holding[i], max(1, left * weights[i] // whole), rest)
            holding[i] = holding[i] + addition
            rest = rest - addition
    return np.array(holding)


def setup_inputs(seed: int = 0) -> dict:
    key_of = jax.random.split(jax.random.key(seed), 5)
    parent_nodes = draw_parent_nodes(jax.random.fold_in(key_of[4], 71), 0)
    marks = draw_marks(jax.random.fold_in(key_of[4], 71), 0)
    child_owner_keys = jax.random.split(jax.random.fold_in(key_of[2], 1), KIDS_ALL // KIDS)
    child_owner_turns = jax.random.permutation(jax.random.fold_in(key_of[2], 3), KIDS_ALL // KIDS)
    child_owner = jax.vmap(lambda own, number: routed_block(jax.random.fold_in(key_of[2], 2), own, number, KIDS, N_SEG * N_RANK, 1, CAP, 2))(child_owner_keys, child_owner_turns).reshape((KIDS_ALL, 1))
    face_link = set_ends(jax.random.randint(key_of[3], (SLOTS_ALL, 6), 0, 3 * SLOTS), jax.random.fold_in(key_of[3], 1), 0, (3 * SLOTS) - 1).astype(jnp.int32)
    return {"parent_nodes": parent_nodes, "marks": marks, "child_owner": child_owner, "face_link": face_link}


def gll_tables():
    points = np.array([-1.0, -math.sqrt(3.0 / 7.0), 0.0, math.sqrt(3.0 / 7.0), 1.0])
    weights = np.array([0.1, 49.0 / 90.0, 32.0 / 45.0, 49.0 / 90.0, 0.1])
    barycentric = np.array([1.0 / np.prod([points[j] - points[m] for m in range(5) if m != j]) for j in range(5)])
    slopes = np.zeros((5, 5))
    for i in range(5):
        for j in range(5):
            if i != j:
                slopes[i, j] = barycentric[j] / barycentric[i] / (points[i] - points[j])
        slopes[i, i] = -np.sum(slopes[i])

    def lagrange_at(where):
        table = np.ones((5, 5))
        for a in range(5):
            for j in range(5):
                for m in range(5):
                    if m != j:
                        table[a, j] *= (where[a] - points[m]) / (points[j] - points[m])
        return table

    def blend(value, side):
        return (1.0 - value) / 2.0 if side == 0 else (1.0 + value) / 2.0

    def flat(i, j, k):
        return i * 25 + j * 5 + k
    ends = (0, 4)
    gordon = np.zeros((125, 125))
    for i in range(5):
        for j in range(5):
            for k in range(5):
                r, s, t = (points[i], points[j], points[k])
                target = flat(i, j, k)
                for a in range(2):
                    gordon[target, flat(ends[a], j, k)] += blend(r, a)
                    gordon[target, flat(i, ends[a], k)] += blend(s, a)
                    gordon[target, flat(i, j, ends[a])] += blend(t, a)
                    for b in range(2):
                        gordon[target, flat(ends[a], ends[b], k)] -= blend(r, a) * blend(s, b)
                        gordon[target, flat(ends[a], j, ends[b])] -= blend(r, a) * blend(t, b)
                        gordon[target, flat(i, ends[a], ends[b])] -= blend(s, a) * blend(t, b)
                        for c in range(2):
                            gordon[target, flat(ends[a], ends[b], ends[c])] += blend(r, a) * blend(s, b) * blend(t, c)
    children = np.zeros((8, 125, 125))
    for octant in range(8):
        shifts = [2 * (octant >> 2 & 1) - 1, 2 * (octant >> 1 & 1) - 1, 2 * (octant & 1) - 1]
        tables = [lagrange_at((points + shifts[q]) / 2.0) for q in range(3)]
        children[octant] = np.kron(np.kron(tables[0], tables[1]), tables[2]) @ gordon
    identity = np.eye(5)
    derivs = [np.kron(np.kron(slopes, identity), identity), np.kron(np.kron(identity, slopes), identity), np.kron(np.kron(identity, identity), slopes)]
    deriv_table = np.concatenate([derivs[q].T for q in range(3)], axis=1)
    mass_weights = np.kron(np.kron(weights, weights), weights)
    face_weights = np.kron(weights, weights)
    face_nodes = []
    for side in (0, 4):
        face_nodes.append([flat(side, j, k) for j in range(5) for k in range(5)])
    face_nodes = [face_nodes[0], face_nodes[1]]
    for side in (0, 4):
        face_nodes.append([flat(i, side, k) for i in range(5) for k in range(5)])
    for side in (0, 4):
        face_nodes.append([flat(i, j, side) for i in range(5) for j in range(5)])
    tangents = [(1, 2), (1, 2), (0, 2), (0, 2), (0, 1), (0, 1)]
    boundary = [flat(i, j, k) for i in range(5) for j in range(5) for k in range(5) if i in ends or j in ends or k in ends]
    children_map = children.transpose(2, 0, 1).reshape(125, 1000)
    return (children_map, deriv_table, mass_weights, face_weights, np.array(face_nodes), tangents, np.array(boundary))

def geometry(coords, tables):
    children_map, deriv_table, mass_weights, face_weights, face_nodes, tangents, boundary = tables
    width = coords.shape[0]
    deriv = jnp.dot(coords.reshape(width * 3, 125), jnp.asarray(deriv_table, jnp.float32), precision=lax.Precision.HIGHEST, preferred_element_type=jnp.float32).reshape(width, 3, 3, 125)
    jac = [[deriv[:, c, d, :] for d in range(3)] for c in range(3)]
    determinant = jac[0][0] * (jac[1][1] * jac[2][2] - jac[1][2] * jac[2][1]) - jac[0][1] * (jac[1][0] * jac[2][2] - jac[1][2] * jac[2][0]) + jac[0][2] * (jac[1][0] * jac[2][1] - jac[1][1] * jac[2][0])
    mass = determinant * jnp.asarray(mass_weights, jnp.float32)
    areas = []
    for face in range(6):
        first, second = tangents[face]
        nodes = face_nodes[face]
        along = deriv[:, :, first, :][:, :, nodes]
        across = deriv[:, :, second, :][:, :, nodes]
        normal_x = along[:, 1] * across[:, 2] - along[:, 2] * across[:, 1]
        normal_y = along[:, 2] * across[:, 0] - along[:, 0] * across[:, 2]
        normal_z = along[:, 0] * across[:, 1] - along[:, 1] * across[:, 0]
        length = jnp.sqrt(normal_x * normal_x + normal_y * normal_y + normal_z * normal_z)
        areas.append(length * jnp.asarray(face_weights, jnp.float32))
    return (mass, jnp.stack(areas, axis=1).reshape(width, 150))

def reference(parent_nodes, marks, child_owner, face_link):
    tables = gll_tables()
    devices = N_SEG * N_RANK
    children_map = jnp.asarray(tables[0], jnp.float32)
    rows = (jnp.arange(devices, dtype=jnp.int32)[:, None] * ELEM_DEV + marks).reshape(-1)
    picked = parent_nodes[rows].reshape(devices * MARKED * 3, 125)
    made = jnp.dot(picked, children_map, precision=lax.Precision.HIGHEST, preferred_element_type=jnp.float32)
    made = made.reshape(devices * MARKED, 3, 8, 125).transpose(0, 2, 1, 3).reshape(devices * KIDS, 375)
    owners = child_owner[:, 0].reshape(devices, KIDS)

    def rank_slots(row):
        onehot = (row[:, None] == jnp.arange(devices, dtype=jnp.int32)[None, :]).astype(jnp.int32)
        return lax.optimization_barrier(jnp.sum(jnp.cumsum(onehot, axis=0) * onehot, axis=1)) - 1
    positions = lax.map(rank_slots, owners)
    sources = jnp.arange(devices, dtype=jnp.int32)[:, None]
    target = (owners * SLOTS + sources * CAP + positions).reshape(-1)
    received = jnp.zeros((devices * SLOTS, 375), jnp.float32).at[target].set(made)
    mass, faces = lax.map(lambda block: geometry(block, tables), received.reshape(devices, SLOTS, 375))
    faces_flat = faces.reshape(devices * SLOTS * 6, 25)
    links = face_link.reshape(N_SEG, N_RANK, SLOTS, 6)
    rank_pos = jnp.arange(N_RANK, dtype=jnp.int32)[None, :, None, None]
    seg_pos = jnp.arange(N_SEG, dtype=jnp.int32)[:, None, None, None]
    source_rank = rank_pos + links // SLOTS - 1
    valid = (source_rank >= 0) & (source_rank < N_RANK)
    owner_of = seg_pos * N_RANK + jnp.clip(source_rank, 0, N_RANK - 1)
    faces_idx = jnp.arange(6, dtype=jnp.int32)
    opposite = faces_idx // 2 * 2 + 1 - faces_idx % 2
    index = ((owner_of * SLOTS + links % SLOTS) * 6 + opposite[None, None, None, :]).reshape(-1)
    fetched = faces_flat[index].reshape(devices * SLOTS, 6, 25)
    fetched = jnp.where(valid.reshape(devices * SLOTS, 6, 1), fetched, jnp.zeros_like(fetched))
    face_total = faces.reshape(devices * SLOTS, 6, 25) + fetched
    return (mass.reshape(devices * SLOTS, 125).T, face_total.reshape(devices * SLOTS, 150).T)
```

```python
import math

import jax
import jax.numpy as jnp
import ml_dtypes
import numpy as np
from jax import lax
from jax.experimental import pallas as pl
from jax.experimental.pallas import tpu as pltpu
from jax.sharding import PartitionSpec as P


def shifted(array, axis, by):
    count = lax.axis_size(axis)
    pairs = [(i, i + by) for i in range(count) if 0 <= i + by < count]
    return lax.ppermute(array, axis, pairs)


def gll_tables():
    points = np.array([-1.0, -math.sqrt(3.0 / 7.0), 0.0, math.sqrt(3.0 / 7.0), 1.0])
    weights = np.array([0.1, 49.0 / 90.0, 32.0 / 45.0, 49.0 / 90.0, 0.1])
    barycentric = np.array(
        [1.0 / np.prod([points[j] - points[m] for m in range(5) if m != j]) for j in range(5)]
    )
    slopes = np.zeros((5, 5))
    for i in range(5):
        for j in range(5):
            if i != j:
                slopes[i, j] = barycentric[j] / barycentric[i] / (points[i] - points[j])
        slopes[i, i] = -np.sum(slopes[i])

    def lagrange_at(where):
        table = np.ones((5, 5))
        for a in range(5):
            for j in range(5):
                for m in range(5):
                    if m != j:
                        table[a, j] *= (where[a] - points[m]) / (points[j] - points[m])
        return table

    def blend(value, side):
        return (1.0 - value) / 2.0 if side == 0 else (1.0 + value) / 2.0

    def flat(i, j, k):
        return i * 25 + j * 5 + k

    ends = (0, 4)
    gordon = np.zeros((125, 125))
    for i in range(5):
        for j in range(5):
            for k in range(5):
                r, s, t = (points[i], points[j], points[k])
                target = flat(i, j, k)
                for a in range(2):
                    gordon[target, flat(ends[a], j, k)] += blend(r, a)
                    gordon[target, flat(i, ends[a], k)] += blend(s, a)
                    gordon[target, flat(i, j, ends[a])] += blend(t, a)
                    for b in range(2):
                        gordon[target, flat(ends[a], ends[b], k)] -= blend(r, a) * blend(s, b)
                        gordon[target, flat(ends[a], j, ends[b])] -= blend(r, a) * blend(t, b)
                        gordon[target, flat(i, ends[a], ends[b])] -= blend(s, a) * blend(t, b)
                        for c in range(2):
                            gordon[target, flat(ends[a], ends[b], ends[c])] += (
                                blend(r, a) * blend(s, b) * blend(t, c)
                            )
    identity = np.eye(5)
    derivs = [
        np.kron(np.kron(slopes, identity), identity),
        np.kron(np.kron(identity, slopes), identity),
        np.kron(np.kron(identity, identity), slopes),
    ]
    mass_weights = np.kron(np.kron(weights, weights), weights)
    face_weights = np.kron(weights, weights)
    tangents = [(1, 2), (1, 2), (0, 2), (0, 2), (0, 1), (0, 1)]
    boundary = [
        flat(i, j, k)
        for i in range(5)
        for j in range(5)
        for k in range(5)
        if i in ends or j in ends or k in ends
    ]
    halves = [lagrange_at((points - 1.0) / 2.0), lagrange_at((points + 1.0) / 2.0)]
    steps = [
        [np.kron(np.kron(half, identity), identity) @ gordon for half in halves],
        [np.kron(np.kron(identity, half), identity) for half in halves],
        [np.kron(np.kron(identity, identity), half) for half in halves],
    ]
    nodes = []
    for side in (0, 4):
        nodes.append([flat(side, j, k) for j in range(5) for k in range(5)])
    for side in (0, 4):
        nodes.append([flat(i, side, k) for i in range(5) for k in range(5)])
    for side in (0, 4):
        nodes.append([flat(i, j, side) for i in range(5) for j in range(5)])
    corners = [flat(i, j, k) for i in ends for j in ends for k in ends]
    return (steps, derivs, mass_weights, face_weights, nodes, tangents, boundary, corners)


HELD = 104
OWNERS = 3 * HELD
WIDTH = 256
NT = (((1,), (1,)), ((), ()))


def parts_of(table):
    high = table.astype(ml_dtypes.bfloat16)
    low = (table - high.astype(np.float64)).astype(ml_dtypes.bfloat16)
    return jnp.asarray(np.concatenate([high, high, low], axis=1))


def padded(table, rows, columns):
    out = np.zeros((rows, columns))
    out[: table.shape[0], : table.shape[1]] = table
    return out


def operators():
    steps, derivs, mass_weights, face_weights, nodes, tangents, boundary, corners = gll_tables()
    pick = np.zeros((OWNERS, 375))
    for c in range(3):
        for row, node in enumerate(boundary):
            pick[c * HELD + row, c * 125 + node] += 1.0
            for corner in corners:
                pick[c * HELD + row, c * 125 + corner] -= 0.125
    first = np.concatenate([padded(step[:, boundary], 128, HELD) for step in steps[0]])
    second = np.concatenate([padded(step, 128, 128) for step in steps[1]])
    third = np.concatenate([padded(step, 128, 128) for step in steps[2]])
    rows = [padded(derivs[0] * mass_weights[:, None], 128, 128)]
    rows += [padded(derivs[d], 128, 128) for d in (1, 2)]
    along = [derivs[tangents[f][0]][nodes[f]] * face_weights[:, None] for f in range(6)]
    across = [derivs[tangents[f][1]][nodes[f]] for f in range(6)]
    rows += [padded(np.concatenate(part), 152, 128) for part in (along, across)]
    return pick, [parts_of(table) for table in (first, second, third, np.concatenate(rows))]


def stacked(values):
    high = values.astype(jnp.bfloat16)
    low = (values - high.astype(jnp.float32)).astype(jnp.bfloat16)
    return jnp.concatenate([high, low, high], axis=0)


def geometry_kernel(cap, block_ref, mask_ref, a1_ref, a2_ref, a3_ref, ad_ref, mass_ref, face_ref, place_ref):
    step = pl.program_id(0)
    group = WIDTH // cap
    f32 = jnp.float32

    @pl.when(step == 0)
    def _():
        row = lax.broadcasted_iota(jnp.int32, (256, 256), 0)
        column = lax.broadcasted_iota(jnp.int32, (256, 256), 1)
        earlier = (row < column).astype(f32).astype(jnp.bfloat16)
        same = (row // 8 == column // 8).astype(f32).astype(jnp.bfloat16)
        within = ((row // 8 == column // 8) & (column < row)).astype(f32).astype(jnp.bfloat16)
        for chunk in range(mask_ref.shape[0] // 256):
            mask = mask_ref[chunk * 256 : (chunk + 1) * 256, :]
            small = mask.astype(jnp.bfloat16)
            before = jnp.dot(small, earlier, preferred_element_type=f32).astype(jnp.bfloat16)
            count = jnp.dot(same, before, preferred_element_type=f32)
            count += jnp.dot(within, small, preferred_element_type=f32)
            place_ref[chunk * 256 : (chunk + 1) * 256, :] = jnp.where(mask > 0.5, count, -1e6)

    span = cap if cap % 128 == 0 else WIDTH
    slot = lax.broadcasted_iota(jnp.int32, (span, 256), 0).astype(f32)
    gathered, octants = [], []
    for s in range(group):
        places = place_ref[pl.ds(pl.multiple_of((step * group + s) * 8, 8), 8), :]
        if span != cap:
            places = places + float(s * cap)
        hit = jnp.zeros((span, 256), f32)
        for o in range(8):
            hit = jnp.where(places[o : o + 1, :] == slot, float(o + 1), hit)
        block = block_ref[s, :OWNERS, :]
        high = block.astype(jnp.bfloat16).astype(f32)
        both = jnp.concatenate([high, block - high], axis=0).astype(jnp.bfloat16)
        chosen = jnp.where(hit > 0.5, 1.0, 0.0).astype(jnp.bfloat16)
        gathered.append(lax.dot_general(both, chosen, NT, preferred_element_type=f32))
        octants.append(
            lax.dot_general(
                jnp.ones((8, 256), jnp.bfloat16), hit.astype(jnp.bfloat16), NT, preferred_element_type=f32
            )
        )
    if span == cap:
        held = jnp.concatenate(gathered, axis=1)
        octant = jnp.concatenate(octants, axis=1)
    else:
        held = sum(gathered[1:], gathered[0])
        octant = sum(octants[1:], octants[0])
    octant = octant[0:1, :]
    bits = []
    for size in (4.0, 2.0, 1.0):
        bit = jnp.where(octant > size + 0.5, 1.0, 0.0)
        octant = octant - size * bit
        bits.append(jnp.concatenate([bit, bit, bit], axis=1))
    high = jnp.concatenate([held[c * HELD : (c + 1) * HELD] for c in range(3)], axis=1)
    low = jnp.concatenate([held[(c + 3) * HELD : (c + 4) * HELD] for c in range(3)], axis=1)
    operand = jnp.concatenate([high, low, high], axis=0).astype(jnp.bfloat16)
    for table_ref, bit in zip((a1_ref, a2_ref, a3_ref), bits):
        sides = jnp.dot(table_ref[...], operand, preferred_element_type=f32)
        operand = stacked(jnp.where(bit > 0.5, sides[128:], sides[:128]))

    def components(start, rows):
        table = ad_ref[start : start + rows, :]
        values = jnp.dot(table, operand, preferred_element_type=f32)
        return [values[:, c * WIDTH : (c + 1) * WIDTH] for c in range(3)]

    def crossed(p, q):
        return [p[1] * q[2] - p[2] * q[1], p[2] * q[0] - p[0] * q[2], p[0] * q[1] - p[1] * q[0]]

    first, second, third = (components(128 * d, 128) for d in range(3))
    normal = crossed(second, third)
    mass_ref[...] = (first[0] * normal[0] + first[1] * normal[1] + first[2] * normal[2])[:125]
    normal = crossed(components(384, 152), components(536, 152))
    face_ref[...] = jnp.sqrt(normal[0] * normal[0] + normal[1] * normal[1] + normal[2] * normal[2])


def whole_spec(array):
    return pl.BlockSpec(array.shape, lambda i: (0,) * array.ndim)


def geometry(blocks, mask, tables, cap):
    devices = blocks.shape[0]
    slots = devices * cap
    group = WIDTH // cap
    return pl.pallas_call(
        lambda *refs: geometry_kernel(cap, *refs),
        grid=(slots // WIDTH,),
        in_specs=[pl.BlockSpec((group,) + blocks.shape[1:], lambda i: (i, 0, 0)), whole_spec(mask)]
        + [whole_spec(table) for table in tables],
        out_specs=[
            pl.BlockSpec((125, WIDTH), lambda i: (0, i)),
            pl.BlockSpec((152, WIDTH), lambda i: (0, i)),
        ],
        out_shape=[
            jax.ShapeDtypeStruct((125, slots), jnp.float32),
            jax.ShapeDtypeStruct((152, slots), jnp.float32),
        ],
        scratch_shapes=[pltpu.VMEM(mask.shape, jnp.float32)],
        compiler_params=pltpu.CompilerParams(vmem_limit_bytes=48 * 1024 * 1024),
        name="geometry",
    )(blocks, mask, *tables)


def assemble_kernel(link_ref, before_ref, own_ref, after_ref, out_ref, low_ref, high_ref, row_low, row_high):
    slots = own_ref.shape[1]
    for part, ref in enumerate((before_ref, own_ref, after_ref)):

        @pl.loop(0, slots // 128)
        def _(number):
            start = pl.multiple_of(number * 128, 128)
            rows = pl.ds(pl.multiple_of(part * slots + number * 128, 128), 128)
            low_ref[rows, :] = ref[0:128, pl.ds(start, 128)].T
            high_ref[rows, :] = ref[24:152, pl.ds(start, 128)].T

    lane = lax.broadcasted_iota(jnp.int32, (1, 128), 1)
    under = [lane < 25 * (g + 1) for g in range(4)]

    @pl.loop(0, slots // 128)
    def _(number):
        start = pl.multiple_of(number * 128, 128)

        @pl.loop(0, 128, step=16)
        def _(inner):
            for k in range(16):
                u = start + inner + k
                row = [link_ref[f * slots + u] for f in range(6)]
                value = low_ref[pl.ds(row[5], 1), :]
                for g in (3, 2, 1, 0):
                    value = jnp.where(under[g], low_ref[pl.ds(row[g ^ 1], 1), :], value)
                row_low[pl.ds(inner + k, 1), :] = value
                row_high[pl.ds(inner + k, 1), :] = high_ref[pl.ds(row[4], 1), :]

        low = row_low[...].T
        high = row_high[...].T
        fetched = [low[25 * (f ^ 1) : 25 * (f ^ 1) + 25] for f in range(4)]
        fetched += [high[101:126], low[100:125]]
        total = own_ref[0:150, pl.ds(start, 128)] + jnp.concatenate(fetched, axis=0)
        out_ref[:, pl.ds(start, 128)] = total


def assemble(link, before, own, after):
    slots = own.shape[1]
    vmem = pl.BlockSpec(memory_space=pltpu.VMEM)
    return pl.pallas_call(
        assemble_kernel,
        in_specs=[pl.BlockSpec(memory_space=pltpu.SMEM), vmem, vmem, vmem],
        out_specs=vmem,
        out_shape=jax.ShapeDtypeStruct((150, slots), jnp.float32),
        scratch_shapes=[
            pltpu.VMEM((3 * slots, 128), jnp.float32),
            pltpu.VMEM((3 * slots, 128), jnp.float32),
            pltpu.VMEM((128, 128), jnp.float32),
            pltpu.VMEM((128, 128), jnp.float32),
        ],
        compiler_params=pltpu.CompilerParams(vmem_limit_bytes=48 * 1024 * 1024),
        name="assemble",
    )(link, before, own, after)


def body(parent_nodes, marks, child_owner, face_link):
    pick, tables = operators()
    devices = lax.axis_size("seg") * lax.axis_size("rank")
    me = lax.axis_index("seg") * lax.axis_size("rank") + lax.axis_index("rank")
    kids = child_owner.shape[0]
    cap = max(2, 2 * kids // devices)
    picked = parent_nodes[marks[0]]
    coords = lax.dot_general(
        jnp.asarray(pick, jnp.float32),
        picked,
        NT,
        precision=lax.Precision.HIGHEST,
        preferred_element_type=jnp.float32,
    )
    owners = child_owner.reshape(kids // 8, 8).T.astype(jnp.float32)
    block = jnp.concatenate([coords, owners], axis=0)
    blocks = lax.all_gather(block, ("seg", "rank"))
    mask = (blocks[:, OWNERS:, :] == me.astype(jnp.float32)).astype(jnp.float32)
    mass, faces = geometry(blocks, mask.reshape(devices * 8, kids // 8), tables, cap)
    before = shifted(faces, "rank", 1)
    after = shifted(faces, "rank", -1)
    return (mass, assemble(face_link.T.reshape(-1), before, faces, after))


def solution(mesh):
    return jax.shard_map(
        body,
        mesh=mesh,
        in_specs=(
            P(("seg", "rank"), None),
            P(("seg", "rank"), None),
            P(("seg", "rank"), None),
            P(("seg", "rank"), None),
        ),
        out_specs=(P(None, ("seg", "rank")), P(None, ("seg", "rank"))),
        check_vma=False,
    )
```

```python
import functools
import math

import jax
import jax.numpy as jnp
import ml_dtypes
import numpy as np
from jax import lax
from jax.experimental import pallas as pl
from jax.experimental.pallas import tpu as pltpu
from jax.sharding import PartitionSpec as P


def shifted(array, axis, by):
    count = lax.axis_size(axis)
    pairs = [(i, i + by) for i in range(count) if 0 <= i + by < count]
    return lax.ppermute(array, axis, pairs)


def gll_tables():
    points = np.array([-1.0, -math.sqrt(3.0 / 7.0), 0.0, math.sqrt(3.0 / 7.0), 1.0])
    weights = np.array([0.1, 49.0 / 90.0, 32.0 / 45.0, 49.0 / 90.0, 0.1])
    barycentric = np.array(
        [1.0 / np.prod([points[j] - points[m] for m in range(5) if m != j]) for j in range(5)]
    )
    slopes = np.zeros((5, 5))
    for i in range(5):
        for j in range(5):
            if i != j:
                slopes[i, j] = barycentric[j] / barycentric[i] / (points[i] - points[j])
        slopes[i, i] = -np.sum(slopes[i])

    def lagrange_at(where):
        table = np.ones((5, 5))
        for a in range(5):
            for j in range(5):
                for m in range(5):
                    if m != j:
                        table[a, j] *= (where[a] - points[m]) / (points[j] - points[m])
        return table

    def blend(value, side):
        return (1.0 - value) / 2.0 if side == 0 else (1.0 + value) / 2.0

    def flat(i, j, k):
        return i * 25 + j * 5 + k

    ends = (0, 4)
    gordon = np.zeros((125, 125))
    for i in range(5):
        for j in range(5):
            for k in range(5):
                r, s, t = (points[i], points[j], points[k])
                target = flat(i, j, k)
                for a in range(2):
                    gordon[target, flat(ends[a], j, k)] += blend(r, a)
                    gordon[target, flat(i, ends[a], k)] += blend(s, a)
                    gordon[target, flat(i, j, ends[a])] += blend(t, a)
                    for b in range(2):
                        gordon[target, flat(ends[a], ends[b], k)] -= blend(r, a) * blend(s, b)
                        gordon[target, flat(ends[a], j, ends[b])] -= blend(r, a) * blend(t, b)
                        gordon[target, flat(i, ends[a], ends[b])] -= blend(s, a) * blend(t, b)
                        for c in range(2):
                            gordon[target, flat(ends[a], ends[b], ends[c])] += (
                                blend(r, a) * blend(s, b) * blend(t, c)
                            )
    identity = np.eye(5)
    derivs = [
        np.kron(np.kron(slopes, identity), identity),
        np.kron(np.kron(identity, slopes), identity),
        np.kron(np.kron(identity, identity), slopes),
    ]
    mass_weights = np.kron(np.kron(weights, weights), weights)
    face_weights = np.kron(weights, weights)
    tangents = [(1, 2), (1, 2), (0, 2), (0, 2), (0, 1), (0, 1)]
    boundary = [
        flat(i, j, k)
        for i in range(5)
        for j in range(5)
        for k in range(5)
        if i in ends or j in ends or k in ends
    ]
    halves = [lagrange_at((points - 1.0) / 2.0), lagrange_at((points + 1.0) / 2.0)]
    steps = [
        [np.kron(np.kron(half, identity), identity) @ gordon for half in halves],
        [np.kron(np.kron(identity, half), identity) for half in halves],
        [np.kron(np.kron(identity, identity), half) for half in halves],
    ]
    nodes = []
    for side in (0, 4):
        nodes.append([flat(side, j, k) for j in range(5) for k in range(5)])
    for side in (0, 4):
        nodes.append([flat(i, side, k) for i in range(5) for k in range(5)])
    for side in (0, 4):
        nodes.append([flat(i, j, side) for i in range(5) for j in range(5)])
    corners = [flat(i, j, k) for i in ends for j in ends for k in ends]
    return (steps, derivs, mass_weights, face_weights, nodes, tangents, boundary, corners)


HELD = 104
OWNERS = 3 * HELD
WIDTH = 256
NT = (((1,), (1,)), ((), ()))


def parts_of(table):
    high = table.astype(ml_dtypes.bfloat16)
    low = (table - high.astype(np.float64)).astype(ml_dtypes.bfloat16)
    return jnp.asarray(np.concatenate([high, high, low], axis=1))


def padded(table, rows, columns):
    out = np.zeros((rows, columns))
    out[: table.shape[0], : table.shape[1]] = table
    return out


def operators():
    steps, derivs, mass_weights, face_weights, nodes, tangents, boundary, corners = gll_tables()
    pick = np.zeros((OWNERS, 375))
    for c in range(3):
        for row, node in enumerate(boundary):
            pick[c * HELD + row, c * 125 + node] += 1.0
            for corner in corners:
                pick[c * HELD + row, c * 125 + corner] -= 0.125
    first = np.concatenate([padded(step[:, boundary], 128, HELD) for step in steps[0]])
    second = np.concatenate([padded(step, 128, 128) for step in steps[1]])
    third = np.concatenate([padded(step, 128, 128) for step in steps[2]])
    rows = [padded(derivs[0] * mass_weights[:, None], 128, 128)]
    rows += [padded(derivs[d], 128, 128) for d in (1, 2)]
    along = [derivs[tangents[f][0]][nodes[f]] * face_weights[:, None] for f in range(6)]
    across = [derivs[tangents[f][1]][nodes[f]] for f in range(6)]
    rows += [padded(np.concatenate(part), 152, 128) for part in (along, across)]
    earlier = jnp.asarray(np.triu(np.ones((256, 256)), 1).astype(ml_dtypes.bfloat16))
    return pick, [earlier] + [parts_of(table) for table in (first, second, third, np.concatenate(rows))]


def stacked(values):
    high = values.astype(jnp.bfloat16)
    low = (values - high.astype(jnp.float32)).astype(jnp.bfloat16)
    return jnp.concatenate([high, low, high], axis=0)


def octant_bits(octant):
    bits = []
    for size in (4.0, 2.0, 1.0):
        bit = jnp.where(octant > size + 0.5, 1.0, 0.0)
        octant = octant - size * bit
        bits.append(jnp.concatenate([bit, bit, bit], axis=1))
    return bits


def chosen_children(block, keys, span):
    f32 = jnp.float32
    slot = lax.broadcasted_iota(jnp.int32, (span, 256), 0).astype(f32)
    hit = jnp.zeros((span, 256), f32)
    for o in range(8):
        hit = jnp.where(keys[o] == slot, float(o + 1), hit)
    high = block.astype(jnp.bfloat16).astype(f32)
    both = jnp.concatenate([high, block - high], axis=0).astype(jnp.bfloat16)
    chosen = jnp.where(hit > 0.5, 1.0, 0.0).astype(jnp.bfloat16)
    held = lax.dot_general(both, chosen, NT, preferred_element_type=f32)
    octant = lax.dot_general(
        jnp.ones((8, 256), jnp.bfloat16), hit.astype(jnp.bfloat16), NT, preferred_element_type=f32
    )
    return held, octant


def masses(held, octant, a1_ref, a2_ref, a3_ref, ad_ref):
    f32 = jnp.float32
    bits = octant_bits(octant[0:1, :])
    high = jnp.concatenate([held[c * HELD : (c + 1) * HELD] for c in range(3)], axis=1)
    low = jnp.concatenate([held[(c + 3) * HELD : (c + 4) * HELD] for c in range(3)], axis=1)
    operand = jnp.concatenate([high, low, high], axis=0).astype(jnp.bfloat16)
    for table_ref, bit in zip((a1_ref, a2_ref, a3_ref), bits):
        sides = jnp.dot(table_ref[...], operand, preferred_element_type=f32)
        operand = stacked(jnp.where(bit > 0.5, sides[128:], sides[:128]))

    def components(start, rows):
        table = ad_ref[start : start + rows, :]
        values = jnp.dot(table, operand, preferred_element_type=f32)
        return [values[:, c * WIDTH : (c + 1) * WIDTH] for c in range(3)]

    def crossed(p, q):
        return [p[1] * q[2] - p[2] * q[1], p[2] * q[0] - p[0] * q[2], p[0] * q[1] - p[1] * q[0]]

    first, second, third = (components(128 * d, 128) for d in range(3))
    normal = crossed(second, third)
    mass = (first[0] * normal[0] + first[1] * normal[1] + first[2] * normal[2])[:125]
    normal = crossed(components(384, 152), components(536, 152))
    face = jnp.sqrt(normal[0] * normal[0] + normal[1] * normal[1] + normal[2] * normal[2])
    return mass, face


def keys_of(mask, earlier):
    before = jnp.dot(mask.astype(jnp.bfloat16), earlier, preferred_element_type=jnp.float32)
    total = jnp.sum(before, axis=0, keepdims=True)
    keys = []
    for o in range(8):
        row = mask[o : o + 1, :]
        keys.append(jnp.where(row > 0.5, total, -1e6))
        total = total + row
    return keys


def geometry_kernel(cap, block_ref, mask_ref, earlier_ref, a1_ref, a2_ref, a3_ref, ad_ref, mass_ref, face_ref):
    gathered, octants = [], []
    aligned = cap % 128 == 0
    for s in range(WIDTH // cap):
        keys = keys_of(mask_ref[s], earlier_ref[...])
        if not aligned:
            keys = [key + float(s * cap) for key in keys]
        held, octant = chosen_children(block_ref[s, :OWNERS, :], keys, cap if aligned else WIDTH)
        gathered.append(held)
        octants.append(octant)
    if aligned:
        held = jnp.concatenate(gathered, axis=1)
        octant = jnp.concatenate(octants, axis=1)
    else:
        held = sum(gathered[1:], gathered[0])
        octant = sum(octants[1:], octants[0])
    mass, face = masses(held, octant, a1_ref, a2_ref, a3_ref, ad_ref)
    mass_ref[...] = mass
    face_ref[...] = face


def whole_spec(array):
    return pl.BlockSpec(array.shape, lambda i: (0,) * array.ndim)


def geometry(blocks, mask, tables, cap):
    devices = blocks.shape[0]
    slots = devices * cap
    group = WIDTH // cap
    return pl.pallas_call(
        lambda *refs: geometry_kernel(cap, *refs),
        grid=(slots // WIDTH,),
        in_specs=[
            pl.BlockSpec((group,) + blocks.shape[1:], lambda i: (i, 0, 0)),
            pl.BlockSpec((group,) + mask.shape[1:], lambda i: (i, 0, 0)),
        ]
        + [whole_spec(table) for table in tables],
        out_specs=[
            pl.BlockSpec((125, WIDTH), lambda i: (0, i)),
            pl.BlockSpec((152, WIDTH), lambda i: (0, i)),
        ],
        out_shape=[
            jax.ShapeDtypeStruct((125, slots), jnp.float32),
            jax.ShapeDtypeStruct((152, slots), jnp.float32),
        ],
        compiler_params=pltpu.CompilerParams(vmem_limit_bytes=48 * 1024 * 1024),
        name="geometry",
    )(blocks, mask, *tables)


MESH = pl.DeviceIdType.MESH
CHIP_Z = 4


def gather_kernel(
    block_ref, earlier_ref, a1_ref, a2_ref, a3_ref, ad_ref,
    mass_ref, face_ref, before_ref, after_ref, held_ref,
    send_up, send_down, send_x, send_y, send_dx, send_dy, send_c, send_next, send_prev,
    recv_z, recv_x, recv_y, recv_dx, recv_dy, recv_c, recv_before, recv_after,
):
    s = lax.axis_index("seg")
    rank = lax.axis_index("rank")
    z, core = rank // 2, rank % 2
    me = s * (2 * CHIP_Z) + rank
    rows = block_ref.shape[0]
    half = rows // 2
    sx = s + 1 - 2 * (s % 2)
    sy = s + 2 - 4 * (s // 2)
    sd = sx + sy - s
    at_x, at_y, at_c = (sx, rank), (sy, rank), (s, rank + 1 - 2 * core)
    above, below = (s, rank + 2), (s, rank - 2)
    next_one, prev_one = (s, rank + 1), (s, rank - 1)
    has_above, has_below = z < CHIP_Z - 1, z > 0
    has_next, has_prev = rank < 2 * CHIP_Z - 1, rank > 0
    step_away = (core == 1) & has_next | (core == 0) & has_prev
    away = (s, rank + 2 * core - 1)

    def number(seg, level):
        return (seg * CHIP_Z + level) * 2 + core

    def level_of(j):
        low = z // 2
        near = jnp.where(j == 0, z, z + 1 - 2 * (z % 2))
        far = jnp.where(low == 0, j, 3 - j)
        return jnp.where(j < 2, near, far)

    def remote(src, dst, send, recv, target):
        return pltpu.make_async_remote_copy(
            src_ref=src, dst_ref=dst, send_sem=send, recv_sem=recv, device_id=target, device_id_type=MESH
        )

    def whole(seg, level, send, recv, target):
        place = held_ref.at[number(seg, level)]
        return remote(place, place, send, recv, target)

    def up(level):
        return whole(s, level, send_up.at[level], recv_z.at[level], above)

    def down(level):
        return whole(s, level, send_down.at[level], recv_z.at[level], below)

    def to_x(level):
        return whole(s, level, send_x.at[level], recv_x.at[level], at_x)

    def to_y(level):
        return whole(s, level, send_y.at[level], recv_y.at[level], at_y)

    def half_to_y(level):
        place = held_ref.at[number(sx, level), pl.ds(0, half)]
        return remote(place, place, send_dy.at[level], recv_dy.at[level], at_y)

    def half_to_x(level):
        place = held_ref.at[number(sy, level), pl.ds(half, half)]
        return remote(place, place, send_dx.at[level], recv_dx.at[level], at_x)

    def to_core(seg, level):
        chip = seg * CHIP_Z + level
        return whole(seg, level, send_c.at[chip], recv_c.at[chip], at_c)

    def from_core(chip):
        place = held_ref.at[chip * 2 + 1 - core]
        return remote(place, place, send_c.at[chip], recv_c.at[chip], at_c)

    def from_x(level):
        return whole(sx, level, send_x.at[level], recv_x.at[level], at_x)

    def from_y(level):
        return whole(sy, level, send_y.at[level], recv_y.at[level], at_y)

    def half_from_y(level):
        place = held_ref.at[number(sd, level), pl.ds(0, half)]
        return remote(place, place, send_dy.at[level], recv_dy.at[level], at_y)

    def half_from_x(level):
        place = held_ref.at[number(sd, level), pl.ds(half, half)]
        return remote(place, place, send_dx.at[level], recv_dx.at[level], at_x)

    def piece(ref, chip):
        return ref.at[:, pl.ds(pl.multiple_of(chip * WIDTH, WIDTH), WIDTH)]

    def to_next(chip):
        return remote(
            piece(face_ref, chip), piece(before_ref, chip), send_next.at[chip], recv_before.at[chip], next_one
        )

    def to_prev(chip):
        return remote(
            piece(face_ref, chip), piece(after_ref, chip), send_prev.at[chip], recv_after.at[chip], prev_one
        )

    barrier = pltpu.get_barrier_semaphore()

    def greet(target):
        pl.semaphore_signal(barrier, inc=1, device_id=target, device_id_type=MESH)

    for target in (at_x, at_y, at_c):
        greet(target)
    for present, target in ((has_above, above), (has_below, below), (step_away, away)):
        pl.when(present)(functools.partial(greet, target))
    held_ref[me] = block_ref[...]
    peers = 3 + sum(present.astype(jnp.int32) for present in (has_above, has_below, step_away))
    pl.semaphore_wait(barrier, peers)

    def spread(level):
        pl.when(has_above & (level <= z))(lambda: up(level).start())
        pl.when(has_below & (level >= z))(lambda: down(level).start())
        to_x(level).start()
        to_y(level).start()
        to_core(s, level).start()

    spread(z)

    @pl.when(rank == 0)
    def _():
        before_ref[...] = jnp.zeros_like(before_ref)

    @pl.when(rank == 2 * CHIP_Z - 1)
    def _():
        after_ref[...] = jnp.zeros_like(after_ref)

    own = me.astype(jnp.float32)

    @pl.loop(0, CHIP_Z + 1)
    def _(j):
        @pl.when(j < CHIP_Z - 1)
        def _():
            level = level_of(j + 1)
            whole(s, level, send_up.at[level], recv_z.at[level], at_c).wait_recv()
            spread(level)

        @pl.when(j < CHIP_Z)
        def _():
            level = level_of(j)
            from_x(level).wait_recv()
            half_to_y(level).start()
            to_core(sx, level).start()
            from_y(level).wait_recv()
            half_to_x(level).start()
            to_core(sy, level).start()

        @pl.loop(0, 4)
        def _(q):
            level = level_of(jnp.where(q < 3, j, j - 1))
            seg = jnp.where(q == 0, s, jnp.where(q == 1, sx, jnp.where(q == 2, sy, sd)))
            chip = seg * CHIP_Z + level

            @pl.when((q == 3) & (j > 0))
            def _():
                half_from_x(level).wait_recv()
                half_from_y(level).wait_recv()
                to_core(sd, level).start()

            @pl.when(((q == 3) & (j > 0)) | ((q < 3) & (j < CHIP_Z)))
            def _():
                from_core(chip).wait_recv()
                gathered, octants = [], []
                for c in range(2):
                    block = held_ref[chip * 2 + c]
                    mask = jnp.where(block[OWNERS:, :] == own, 1.0, 0.0)
                    held, octant = chosen_children(block[:OWNERS, :], keys_of(mask, earlier_ref[...]), WIDTH // 2)
                    gathered.append(held)
                    octants.append(octant)
                mass, face = masses(
                    jnp.concatenate(gathered, axis=1), jnp.concatenate(octants, axis=1), a1_ref, a2_ref, a3_ref, ad_ref
                )
                lanes = pl.ds(pl.multiple_of(chip * WIDTH, WIDTH), WIDTH)
                mass_ref[:, lanes] = mass
                face_ref[:, lanes] = face
                pl.when(has_next)(lambda: to_next(chip).start())
                pl.when(has_prev)(lambda: to_prev(chip).start())

    @pl.loop(0, CHIP_Z)
    def _(level):
        pl.when(has_above & (level <= z))(lambda: up(level).wait_send())
        pl.when(has_below & (level >= z))(lambda: down(level).wait_send())
        to_x(level).wait_send()
        to_y(level).wait_send()
        half_to_x(level).wait_send()
        half_to_y(level).wait_send()

    @pl.loop(0, 4 * CHIP_Z)
    def _(chip):
        to_core(chip // CHIP_Z, chip % CHIP_Z).wait_send()

        @pl.when(has_next)
        def _():
            to_next(chip).wait_send()
            remote(
                piece(face_ref, chip), piece(after_ref, chip), send_next.at[chip], recv_after.at[chip], next_one
            ).wait_recv()

        @pl.when(has_prev)
        def _():
            to_prev(chip).wait_send()
            remote(
                piece(face_ref, chip), piece(before_ref, chip), send_prev.at[chip], recv_before.at[chip], prev_one
            ).wait_recv()


def gather_and_compute(block, tables, cap):
    devices = 8 * CHIP_Z
    slots = devices * cap
    vmem = pl.BlockSpec(memory_space=pltpu.VMEM)
    faces = jax.ShapeDtypeStruct((152, slots), jnp.float32)
    dma = pltpu.SemaphoreType.DMA
    chips = 4 * CHIP_Z
    return pl.pallas_call(
        gather_kernel,
        in_specs=[vmem] * (1 + len(tables)),
        out_specs=[vmem] * 4,
        out_shape=[jax.ShapeDtypeStruct((125, slots), jnp.float32), faces, faces, faces],
        scratch_shapes=[pltpu.VMEM((devices,) + block.shape, jnp.float32)]
        + [dma((CHIP_Z,))] * 6
        + [dma((chips,))] * 3
        + [dma((CHIP_Z,))] * 5
        + [dma((chips,))] * 3,
        compiler_params=pltpu.CompilerParams(
            collective_id=0, has_side_effects=True, vmem_limit_bytes=48 * 1024 * 1024
        ),
        name="gather_and_compute",
    )(block, *tables)


def assemble_kernel(link_ref, before_ref, own_ref, after_ref, out_ref, low_ref, high_ref, row_low, row_high):
    slots = own_ref.shape[1]
    for part, ref in enumerate((before_ref, own_ref, after_ref)):

        @pl.loop(0, slots // 128)
        def _(number):
            start = pl.multiple_of(number * 128, 128)
            rows = pl.ds(pl.multiple_of(part * slots + number * 128, 128), 128)
            low_ref[rows, :] = ref[0:128, pl.ds(start, 128)].T
            high_ref[rows, :] = ref[24:152, pl.ds(start, 128)].T

    lane = lax.broadcasted_iota(jnp.int32, (1, 128), 1)
    under = [lane < 25 * (g + 1) for g in range(4)]

    @pl.loop(0, slots // 128)
    def _(number):
        start = pl.multiple_of(number * 128, 128)

        @pl.loop(0, 128, step=16)
        def _(inner):
            for k in range(16):
                u = start + inner + k
                row = [link_ref[f * slots + u] for f in range(6)]
                value = low_ref[pl.ds(row[5], 1), :]
                for g in (3, 2, 1, 0):
                    value = jnp.where(under[g], low_ref[pl.ds(row[g ^ 1], 1), :], value)
                row_low[pl.ds(inner + k, 1), :] = value
                row_high[pl.ds(inner + k, 1), :] = high_ref[pl.ds(row[4], 1), :]

        low = row_low[...].T
        high = row_high[...].T
        fetched = [low[25 * (f ^ 1) : 25 * (f ^ 1) + 25] for f in range(4)]
        fetched += [high[101:126], low[100:125]]
        total = own_ref[0:150, pl.ds(start, 128)] + jnp.concatenate(fetched, axis=0)
        out_ref[:, pl.ds(start, 128)] = total


def assemble(link, before, own, after):
    slots = own.shape[1]
    vmem = pl.BlockSpec(memory_space=pltpu.VMEM)
    return pl.pallas_call(
        assemble_kernel,
        in_specs=[pl.BlockSpec(memory_space=pltpu.SMEM), vmem, vmem, vmem],
        out_specs=vmem,
        out_shape=jax.ShapeDtypeStruct((150, slots), jnp.float32),
        scratch_shapes=[
            pltpu.VMEM((3 * slots, 128), jnp.float32),
            pltpu.VMEM((3 * slots, 128), jnp.float32),
            pltpu.VMEM((128, 128), jnp.float32),
            pltpu.VMEM((128, 128), jnp.float32),
        ],
        compiler_params=pltpu.CompilerParams(vmem_limit_bytes=48 * 1024 * 1024),
        name="assemble",
    )(link, before, own, after)


def body(parent_nodes, marks, child_owner, face_link):
    pick, tables = operators()
    devices = lax.axis_size("seg") * lax.axis_size("rank")
    me = lax.axis_index("seg") * lax.axis_size("rank") + lax.axis_index("rank")
    kids = child_owner.shape[0]
    cap = max(2, 2 * kids // devices)
    picked = parent_nodes[marks[0]]
    coords = lax.dot_general(
        jnp.asarray(pick, jnp.float32),
        picked,
        NT,
        precision=lax.Precision.HIGHEST,
        preferred_element_type=jnp.float32,
    )
    owners = child_owner.reshape(kids // 8, 8).T.astype(jnp.float32)
    block = jnp.concatenate([coords, owners], axis=0)
    if lax.axis_size("seg") == 4 and lax.axis_size("rank") == 2 * CHIP_Z and 2 * cap == WIDTH:
        mass, faces, before, after = gather_and_compute(block, tables, cap)
    else:
        blocks = lax.all_gather(block, ("seg", "rank"))
        mask = (blocks[:, OWNERS:, :] == me.astype(jnp.float32)).astype(jnp.float32)
        mass, faces = geometry(blocks, mask, tables, cap)
        before = shifted(faces, "rank", 1)
        after = shifted(faces, "rank", -1)
    return (mass, assemble(face_link.T.reshape(-1), before, faces, after))


def solution(mesh):
    return jax.shard_map(
        body,
        mesh=mesh,
        in_specs=(
            P(("seg", "rank"), None),
            P(("seg", "rank"), None),
            P(("seg", "rank"), None),
            P(("seg", "rank"), None),
        ),
        out_specs=(P(None, ("seg", "rank")), P(None, ("seg", "rank"))),
        check_vma=False,
    )
```

```python
import functools
import math

import jax
import jax.numpy as jnp
import ml_dtypes
import numpy as np
from jax import lax
from jax.experimental import pallas as pl
from jax.experimental.pallas import tpu as pltpu
from jax.sharding import PartitionSpec as P


def shifted(array, axis, by):
    count = lax.axis_size(axis)
    pairs = [(i, i + by) for i in range(count) if 0 <= i + by < count]
    return lax.ppermute(array, axis, pairs)


def gll_tables():
    points = np.array([-1.0, -math.sqrt(3.0 / 7.0), 0.0, math.sqrt(3.0 / 7.0), 1.0])
    weights = np.array([0.1, 49.0 / 90.0, 32.0 / 45.0, 49.0 / 90.0, 0.1])
    barycentric = np.array(
        [1.0 / np.prod([points[j] - points[m] for m in range(5) if m != j]) for j in range(5)]
    )
    slopes = np.zeros((5, 5))
    for i in range(5):
        for j in range(5):
            if i != j:
                slopes[i, j] = barycentric[j] / barycentric[i] / (points[i] - points[j])
        slopes[i, i] = -np.sum(slopes[i])

    def lagrange_at(where):
        table = np.ones((5, 5))
        for a in range(5):
            for j in range(5):
                for m in range(5):
                    if m != j:
                        table[a, j] *= (where[a] - points[m]) / (points[j] - points[m])
        return table

    def blend(value, side):
        return (1.0 - value) / 2.0 if side == 0 else (1.0 + value) / 2.0

    def flat(i, j, k):
        return i * 25 + j * 5 + k

    ends = (0, 4)
    gordon = np.zeros((125, 125))
    for i in range(5):
        for j in range(5):
            for k in range(5):
                r, s, t = (points[i], points[j], points[k])
                target = flat(i, j, k)
                for a in range(2):
                    gordon[target, flat(ends[a], j, k)] += blend(r, a)
                    gordon[target, flat(i, ends[a], k)] += blend(s, a)
                    gordon[target, flat(i, j, ends[a])] += blend(t, a)
                    for b in range(2):
                        gordon[target, flat(ends[a], ends[b], k)] -= blend(r, a) * blend(s, b)
                        gordon[target, flat(ends[a], j, ends[b])] -= blend(r, a) * blend(t, b)
                        gordon[target, flat(i, ends[a], ends[b])] -= blend(s, a) * blend(t, b)
                        for c in range(2):
                            gordon[target, flat(ends[a], ends[b], ends[c])] += (
                                blend(r, a) * blend(s, b) * blend(t, c)
                            )
    identity = np.eye(5)
    derivs = [
        np.kron(np.kron(slopes, identity), identity),
        np.kron(np.kron(identity, slopes), identity),
        np.kron(np.kron(identity, identity), slopes),
    ]
    mass_weights = np.kron(np.kron(weights, weights), weights)
    face_weights = np.kron(weights, weights)
    tangents = [(1, 2), (1, 2), (0, 2), (0, 2), (0, 1), (0, 1)]
    boundary = [
        flat(i, j, k)
        for i in range(5)
        for j in range(5)
        for k in range(5)
        if i in ends or j in ends or k in ends
    ]
    halves = [lagrange_at((points - 1.0) / 2.0), lagrange_at((points + 1.0) / 2.0)]
    steps = [
        [np.kron(np.kron(half, identity), identity) @ gordon for half in halves],
        [np.kron(np.kron(identity, half), identity) for half in halves],
        [np.kron(np.kron(identity, identity), half) for half in halves],
    ]
    nodes = []
    for side in (0, 4):
        nodes.append([flat(side, j, k) for j in range(5) for k in range(5)])
    for side in (0, 4):
        nodes.append([flat(i, side, k) for i in range(5) for k in range(5)])
    for side in (0, 4):
        nodes.append([flat(i, j, side) for i in range(5) for j in range(5)])
    corners = [flat(i, j, k) for i in ends for j in ends for k in ends]
    return (steps, derivs, mass_weights, face_weights, nodes, tangents, boundary, corners)


HELD = 104
OWNERS = 3 * HELD
WIDTH = 256
NT = (((1,), (1,)), ((), ()))


def parts_of(table):
    high = table.astype(ml_dtypes.bfloat16)
    low = (table - high.astype(np.float64)).astype(ml_dtypes.bfloat16)
    return jnp.asarray(np.concatenate([high, high, low], axis=1))


def padded(table, rows, columns):
    out = np.zeros((rows, columns))
    out[: table.shape[0], : table.shape[1]] = table
    return out


def operators():
    steps, derivs, mass_weights, face_weights, nodes, tangents, boundary, corners = gll_tables()
    pick = np.zeros((OWNERS, 375))
    for c in range(3):
        for row, node in enumerate(boundary):
            pick[c * HELD + row, c * 125 + node] += 1.0
            for corner in corners:
                pick[c * HELD + row, c * 125 + corner] -= 0.125
    first = np.concatenate([padded(step[:, boundary], 128, HELD) for step in steps[0]])
    second = np.concatenate([padded(step, 128, 128) for step in steps[1]])
    third = np.concatenate([padded(step, 128, 128) for step in steps[2]])
    rows = [padded(derivs[0] * mass_weights[:, None], 128, 128)]
    rows += [padded(derivs[d], 128, 128) for d in (1, 2)]
    along = [derivs[tangents[f][0]][nodes[f]] * face_weights[:, None] for f in range(6)]
    across = [derivs[tangents[f][1]][nodes[f]] for f in range(6)]
    rows += [padded(np.concatenate(part), 152, 128) for part in (along, across)]
    earlier = jnp.asarray(np.triu(np.ones((256, 256)), 1).astype(ml_dtypes.bfloat16))
    return pick, [earlier] + [parts_of(table) for table in (first, second, third, np.concatenate(rows))]


def stacked(values):
    high = values.astype(jnp.bfloat16)
    low = (values - high.astype(jnp.float32)).astype(jnp.bfloat16)
    return jnp.concatenate([high, low, high], axis=0)


def octant_bits(octant):
    bits = []
    for size in (4.0, 2.0, 1.0):
        bit = jnp.where(octant > size + 0.5, 1.0, 0.0)
        octant = octant - size * bit
        bits.append(jnp.concatenate([bit, bit, bit], axis=1))
    return bits


def chosen_children(block, keys, span):
    f32 = jnp.float32
    slot = lax.broadcasted_iota(jnp.int32, (span, 256), 0).astype(f32)
    hit = jnp.zeros((span, 256), f32)
    for o in range(8):
        hit = jnp.where(keys[o] == slot, float(o + 1), hit)
    high = block.astype(jnp.bfloat16).astype(f32)
    both = jnp.concatenate([high, block - high], axis=0).astype(jnp.bfloat16)
    chosen = jnp.where(hit > 0.5, 1.0, 0.0).astype(jnp.bfloat16)
    held = lax.dot_general(both, chosen, NT, preferred_element_type=f32)
    octant = lax.dot_general(
        jnp.ones((8, 256), jnp.bfloat16), hit.astype(jnp.bfloat16), NT, preferred_element_type=f32
    )
    return held, octant


def masses(held, octant, a1_ref, a2_ref, a3_ref, ad_ref):
    f32 = jnp.float32
    bits = octant_bits(octant[0:1, :])
    high = jnp.concatenate([held[c * HELD : (c + 1) * HELD] for c in range(3)], axis=1)
    low = jnp.concatenate([held[(c + 3) * HELD : (c + 4) * HELD] for c in range(3)], axis=1)
    operand = jnp.concatenate([high, low, high], axis=0).astype(jnp.bfloat16)
    for table_ref, bit in zip((a1_ref, a2_ref, a3_ref), bits):
        sides = jnp.dot(table_ref[...], operand, preferred_element_type=f32)
        operand = stacked(jnp.where(bit > 0.5, sides[128:], sides[:128]))

    def components(start, rows):
        table = ad_ref[start : start + rows, :]
        values = jnp.dot(table, operand, preferred_element_type=f32)
        return [values[:, c * WIDTH : (c + 1) * WIDTH] for c in range(3)]

    def crossed(p, q):
        return [p[1] * q[2] - p[2] * q[1], p[2] * q[0] - p[0] * q[2], p[0] * q[1] - p[1] * q[0]]

    first, second, third = (components(128 * d, 128) for d in range(3))
    normal = crossed(second, third)
    mass = (first[0] * normal[0] + first[1] * normal[1] + first[2] * normal[2])[:125]
    normal = crossed(components(384, 152), components(536, 152))
    face = jnp.sqrt(normal[0] * normal[0] + normal[1] * normal[1] + normal[2] * normal[2])
    return mass, face


def keys_of(mask, earlier):
    before = jnp.dot(mask.astype(jnp.bfloat16), earlier, preferred_element_type=jnp.float32)
    total = jnp.sum(before, axis=0, keepdims=True)
    keys = []
    for o in range(8):
        row = mask[o : o + 1, :]
        keys.append(jnp.where(row > 0.5, total, -1e6))
        total = total + row
    return keys


def geometry_kernel(cap, block_ref, mask_ref, earlier_ref, a1_ref, a2_ref, a3_ref, ad_ref, mass_ref, face_ref):
    gathered, octants = [], []
    aligned = cap % 128 == 0
    for s in range(WIDTH // cap):
        keys = keys_of(mask_ref[s], earlier_ref[...])
        if not aligned:
            keys = [key + float(s * cap) for key in keys]
        held, octant = chosen_children(block_ref[s, :OWNERS, :], keys, cap if aligned else WIDTH)
        gathered.append(held)
        octants.append(octant)
    if aligned:
        held = jnp.concatenate(gathered, axis=1)
        octant = jnp.concatenate(octants, axis=1)
    else:
        held = sum(gathered[1:], gathered[0])
        octant = sum(octants[1:], octants[0])
    mass, face = masses(held, octant, a1_ref, a2_ref, a3_ref, ad_ref)
    mass_ref[...] = mass
    face_ref[...] = face


def whole_spec(array):
    return pl.BlockSpec(array.shape, lambda i: (0,) * array.ndim)


def geometry(blocks, mask, tables, cap):
    devices = blocks.shape[0]
    slots = devices * cap
    group = WIDTH // cap
    return pl.pallas_call(
        lambda *refs: geometry_kernel(cap, *refs),
        grid=(slots // WIDTH,),
        in_specs=[
            pl.BlockSpec((group,) + blocks.shape[1:], lambda i: (i, 0, 0)),
            pl.BlockSpec((group,) + mask.shape[1:], lambda i: (i, 0, 0)),
        ]
        + [whole_spec(table) for table in tables],
        out_specs=[
            pl.BlockSpec((125, WIDTH), lambda i: (0, i)),
            pl.BlockSpec((152, WIDTH), lambda i: (0, i)),
        ],
        out_shape=[
            jax.ShapeDtypeStruct((125, slots), jnp.float32),
            jax.ShapeDtypeStruct((152, slots), jnp.float32),
        ],
        compiler_params=pltpu.CompilerParams(vmem_limit_bytes=48 * 1024 * 1024),
        name="geometry",
    )(blocks, mask, *tables)


def picked_coords(nodes, marks, pick):
    f32 = jnp.float32
    row = lax.broadcasted_iota(jnp.int32, (nodes.shape[1], marks.shape[1]), 0)
    chosen = jnp.where(row == marks, 1.0, 0.0).astype(jnp.bfloat16)
    coords = None
    for _ in range(3):
        part = nodes.astype(jnp.bfloat16)
        nodes = nodes - part.astype(f32)
        part = jnp.dot(part, chosen, preferred_element_type=f32).astype(jnp.bfloat16)
        part = jnp.dot(pick, part, preferred_element_type=f32)
        coords = part if coords is None else coords + part
    return coords


MESH = pl.DeviceIdType.MESH
CHIP_Z = 4


def gather_kernel(
    nodes_ref, marks_ref, owners_ref, pick_ref, earlier_ref, a1_ref, a2_ref, a3_ref, ad_ref,
    mass_ref, face_ref, before_ref, after_ref, held_ref,
    send_up, send_down, send_x, send_y, send_dx, send_dy, send_c, send_next, send_prev,
    recv_z, recv_x, recv_y, recv_dx, recv_dy, recv_c, recv_before, recv_after,
):
    s = lax.axis_index("seg")
    rank = lax.axis_index("rank")
    z, core = rank // 2, rank % 2
    me = s * (2 * CHIP_Z) + rank
    half = held_ref.shape[1] // 2
    sx = s + 1 - 2 * (s % 2)
    sy = s + 2 - 4 * (s // 2)
    sd = sx + sy - s
    at_x, at_y, at_c = (sx, rank), (sy, rank), (s, rank + 1 - 2 * core)
    above, below = (s, rank + 2), (s, rank - 2)
    next_one, prev_one = (s, rank + 1), (s, rank - 1)
    has_above, has_below = z < CHIP_Z - 1, z > 0
    has_next, has_prev = rank < 2 * CHIP_Z - 1, rank > 0
    step_away = (core == 1) & has_next | (core == 0) & has_prev
    away = (s, rank + 2 * core - 1)

    def number(seg, level):
        return (seg * CHIP_Z + level) * 2 + core

    def level_of(j):
        low = z // 2
        near = jnp.where(j == 0, z, z + 1 - 2 * (z % 2))
        far = jnp.where(low == 0, j, 3 - j)
        return jnp.where(j < 2, near, far)

    def remote(src, dst, send, recv, target):
        return pltpu.make_async_remote_copy(
            src_ref=src, dst_ref=dst, send_sem=send, recv_sem=recv, device_id=target, device_id_type=MESH
        )

    def whole(seg, level, send, recv, target):
        place = held_ref.at[number(seg, level)]
        return remote(place, place, send, recv, target)

    def up(level):
        return whole(s, level, send_up.at[level], recv_z.at[level], above)

    def down(level):
        return whole(s, level, send_down.at[level], recv_z.at[level], below)

    def to_x(level):
        return whole(s, level, send_x.at[level], recv_x.at[level], at_x)

    def to_y(level):
        return whole(s, level, send_y.at[level], recv_y.at[level], at_y)

    def half_to_y(level):
        place = held_ref.at[number(sx, level), pl.ds(0, half)]
        return remote(place, place, send_dy.at[level], recv_dy.at[level], at_y)

    def half_to_x(level):
        place = held_ref.at[number(sy, level), pl.ds(half, half)]
        return remote(place, place, send_dx.at[level], recv_dx.at[level], at_x)

    def to_core(seg, level):
        chip = seg * CHIP_Z + level
        return whole(seg, level, send_c.at[chip], recv_c.at[chip], at_c)

    def from_core(chip):
        place = held_ref.at[chip * 2 + 1 - core]
        return remote(place, place, send_c.at[chip], recv_c.at[chip], at_c)

    def from_x(level):
        return whole(sx, level, send_x.at[level], recv_x.at[level], at_x)

    def from_y(level):
        return whole(sy, level, send_y.at[level], recv_y.at[level], at_y)

    def half_from_y(level):
        place = held_ref.at[number(sd, level), pl.ds(0, half)]
        return remote(place, place, send_dy.at[level], recv_dy.at[level], at_y)

    def half_from_x(level):
        place = held_ref.at[number(sd, level), pl.ds(half, half)]
        return remote(place, place, send_dx.at[level], recv_dx.at[level], at_x)

    def piece(ref, chip):
        return ref.at[:, pl.ds(pl.multiple_of(chip * WIDTH, WIDTH), WIDTH)]

    def to_next(chip):
        return remote(
            piece(face_ref, chip), piece(before_ref, chip), send_next.at[chip], recv_before.at[chip], next_one
        )

    def to_prev(chip):
        return remote(
            piece(face_ref, chip), piece(after_ref, chip), send_prev.at[chip], recv_after.at[chip], prev_one
        )

    barrier = pltpu.get_barrier_semaphore()

    def greet(target):
        pl.semaphore_signal(barrier, inc=1, device_id=target, device_id_type=MESH)

    for target in (at_x, at_y, at_c):
        greet(target)
    for present, target in ((has_above, above), (has_below, below), (step_away, away)):
        pl.when(present)(functools.partial(greet, target))
    held_ref[me, :OWNERS, :] = picked_coords(nodes_ref[...], marks_ref[...], pick_ref[...])
    held_ref[me, OWNERS:, :] = owners_ref[...]
    peers = 3 + sum(present.astype(jnp.int32) for present in (has_above, has_below, step_away))
    pl.semaphore_wait(barrier, peers)

    def spread(level):
        pl.when(has_above & (level <= z))(lambda: up(level).start())
        pl.when(has_below & (level >= z))(lambda: down(level).start())
        to_x(level).start()
        to_y(level).start()
        to_core(s, level).start()

    spread(z)

    @pl.when(rank == 0)
    def _():
        before_ref[...] = jnp.zeros_like(before_ref)

    @pl.when(rank == 2 * CHIP_Z - 1)
    def _():
        after_ref[...] = jnp.zeros_like(after_ref)

    own = me.astype(jnp.float32)

    def along_z(position):
        level = level_of(position)
        whole(s, level, send_up.at[level], recv_z.at[level], at_c).wait_recv()
        spread(level)

    def diagonal(level):
        half_from_x(level).wait_recv()
        half_from_y(level).wait_recv()
        to_core(sd, level).start()

    middle = (has_above & has_below).astype(jnp.int32)

    @pl.loop(0, 4 * CHIP_Z + 2)
    def _(t):
        j, k = (t + 3) // 4 - 1, (t + 3) % 4

        @pl.when((k == 0) & (j >= 0) & (j < CHIP_Z))
        def _():
            pl.when((middle == 1) & (j == 0))(lambda: along_z(1))
            pl.when(j + 1 + middle < CHIP_Z)(lambda: along_z(j + 1 + middle))
            level = level_of(j)
            from_x(level).wait_recv()
            half_to_y(level).start()
            to_core(sx, level).start()
            from_y(level).wait_recv()
            half_to_x(level).start()
            to_core(sy, level).start()

        pl.when((k == 2) & (j >= 1) & (j < CHIP_Z))(lambda: diagonal(level_of(j - 1)))
        pl.when(t == 4 * CHIP_Z + 1)(lambda: diagonal(level_of(CHIP_Z - 1)))
        column = (k == 0) & (j < CHIP_Z - 1) | (t == 0)
        slanted = (k == 3) & (j >= 1) | (t == 4 * CHIP_Z + 1)
        position = jnp.where(t == 0, 0, jnp.where(column, j + 1, jnp.where(slanted, j - 1, j)))
        seg = jnp.where(column, s, jnp.where(slanted, sd, jnp.where(k == 1, sx, sy)))
        chip = seg * CHIP_Z + level_of(position)

        @pl.when(column | slanted | (k == 1) | (k == 2))
        def _():
            from_core(chip).wait_recv()
            gathered, octants = [], []
            for c in range(2):
                block = held_ref[chip * 2 + c]
                mask = jnp.where(block[OWNERS:, :] == own, 1.0, 0.0)
                held, octant = chosen_children(block[:OWNERS, :], keys_of(mask, earlier_ref[...]), WIDTH // 2)
                gathered.append(held)
                octants.append(octant)
            mass, face = masses(
                jnp.concatenate(gathered, axis=1), jnp.concatenate(octants, axis=1), a1_ref, a2_ref, a3_ref, ad_ref
            )
            lanes = pl.ds(pl.multiple_of(chip * WIDTH, WIDTH), WIDTH)
            mass_ref[:, lanes] = mass
            face_ref[:, lanes] = face
            pl.when(has_next)(lambda: to_next(chip).start())
            pl.when(has_prev)(lambda: to_prev(chip).start())

    @pl.loop(0, CHIP_Z)
    def _(level):
        pl.when(has_above & (level <= z))(lambda: up(level).wait_send())
        pl.when(has_below & (level >= z))(lambda: down(level).wait_send())
        to_x(level).wait_send()
        to_y(level).wait_send()
        half_to_x(level).wait_send()
        half_to_y(level).wait_send()

    @pl.loop(0, 4 * CHIP_Z)
    def _(chip):
        to_core(chip // CHIP_Z, chip % CHIP_Z).wait_send()

        @pl.when(has_next)
        def _():
            to_next(chip).wait_send()
            remote(
                piece(face_ref, chip), piece(after_ref, chip), send_next.at[chip], recv_after.at[chip], next_one
            ).wait_recv()

        @pl.when(has_prev)
        def _():
            to_prev(chip).wait_send()
            remote(
                piece(face_ref, chip), piece(before_ref, chip), send_prev.at[chip], recv_before.at[chip], prev_one
            ).wait_recv()


def gather_and_compute(nodes, marks, owners, pick, tables, cap):
    devices = 8 * CHIP_Z
    slots = devices * cap
    vmem = pl.BlockSpec(memory_space=pltpu.VMEM)
    faces = jax.ShapeDtypeStruct((152, slots), jnp.float32)
    dma = pltpu.SemaphoreType.DMA
    chips = 4 * CHIP_Z
    return pl.pallas_call(
        gather_kernel,
        in_specs=[vmem] * (4 + len(tables)),
        out_specs=[vmem] * 4,
        out_shape=[jax.ShapeDtypeStruct((125, slots), jnp.float32), faces, faces, faces],
        scratch_shapes=[pltpu.VMEM((devices, OWNERS + 8, owners.shape[1]), jnp.float32)]
        + [dma((CHIP_Z,))] * 6
        + [dma((chips,))] * 3
        + [dma((CHIP_Z,))] * 5
        + [dma((chips,))] * 3,
        compiler_params=pltpu.CompilerParams(
            collective_id=0, has_side_effects=True, vmem_limit_bytes=48 * 1024 * 1024
        ),
        name="gather_and_compute",
    )(nodes, marks, owners, pick, *tables)


def assemble_kernel(link_ref, before_ref, own_ref, after_ref, out_ref, low_ref, high_ref, row_low, row_high):
    slots = own_ref.shape[1]
    for part, ref in enumerate((before_ref, own_ref, after_ref)):

        @pl.loop(0, slots // 128)
        def _(number):
            start = pl.multiple_of(number * 128, 128)
            rows = pl.ds(pl.multiple_of(part * slots + number * 128, 128), 128)
            low_ref[rows, :] = ref[0:128, pl.ds(start, 128)].T
            high_ref[rows, :] = ref[24:152, pl.ds(start, 128)].T

    lane = lax.broadcasted_iota(jnp.int32, (1, 128), 1)
    under = [lane < 25 * (g + 1) for g in range(4)]

    @pl.loop(0, slots // 128)
    def _(number):
        start = pl.multiple_of(number * 128, 128)

        @pl.loop(0, 128, step=16)
        def _(inner):
            for k in range(16):
                u = start + inner + k
                row = [link_ref[f * slots + u] for f in range(6)]
                value = low_ref[pl.ds(row[5], 1), :]
                for g in (3, 2, 1, 0):
                    value = jnp.where(under[g], low_ref[pl.ds(row[g ^ 1], 1), :], value)
                row_low[pl.ds(inner + k, 1), :] = value
                row_high[pl.ds(inner + k, 1), :] = high_ref[pl.ds(row[4], 1), :]

        low = row_low[...].T
        high = row_high[...].T
        fetched = [low[25 * (f ^ 1) : 25 * (f ^ 1) + 25] for f in range(4)]
        fetched += [high[101:126], low[100:125]]
        total = own_ref[0:150, pl.ds(start, 128)] + jnp.concatenate(fetched, axis=0)
        out_ref[:, pl.ds(start, 128)] = total


def assemble(link, before, own, after):
    slots = own.shape[1]
    vmem = pl.BlockSpec(memory_space=pltpu.VMEM)
    return pl.pallas_call(
        assemble_kernel,
        in_specs=[pl.BlockSpec(memory_space=pltpu.SMEM), vmem, vmem, vmem],
        out_specs=vmem,
        out_shape=jax.ShapeDtypeStruct((150, slots), jnp.float32),
        scratch_shapes=[
            pltpu.VMEM((3 * slots, 128), jnp.float32),
            pltpu.VMEM((3 * slots, 128), jnp.float32),
            pltpu.VMEM((128, 128), jnp.float32),
            pltpu.VMEM((128, 128), jnp.float32),
        ],
        compiler_params=pltpu.CompilerParams(vmem_limit_bytes=48 * 1024 * 1024),
        name="assemble",
    )(link, before, own, after)


def body(parent_nodes, marks, child_owner, face_link):
    pick, tables = operators()
    devices = lax.axis_size("seg") * lax.axis_size("rank")
    me = lax.axis_index("seg") * lax.axis_size("rank") + lax.axis_index("rank")
    kids = child_owner.shape[0]
    cap = max(2, 2 * kids // devices)
    owners = child_owner.reshape(kids // 8, 8).T.astype(jnp.float32)
    if lax.axis_size("seg") == 4 and lax.axis_size("rank") == 2 * CHIP_Z and 2 * cap == WIDTH:
        mass, faces, before, after = gather_and_compute(
            parent_nodes.T, marks, owners, jnp.asarray(pick, jnp.bfloat16), tables, cap
        )
    else:
        coords = lax.dot_general(
            jnp.asarray(pick, jnp.float32),
            parent_nodes[marks[0]],
            NT,
            precision=lax.Precision.HIGHEST,
            preferred_element_type=jnp.float32,
        )
        blocks = lax.all_gather(jnp.concatenate([coords, owners], axis=0), ("seg", "rank"))
        mask = (blocks[:, OWNERS:, :] == me.astype(jnp.float32)).astype(jnp.float32)
        mass, faces = geometry(blocks, mask, tables, cap)
        before = shifted(faces, "rank", 1)
        after = shifted(faces, "rank", -1)
    return (mass, assemble(face_link.T.reshape(-1), before, faces, after))


def solution(mesh):
    return jax.shard_map(
        body,
        mesh=mesh,
        in_specs=(
            P(("seg", "rank"), None),
            P(("seg", "rank"), None),
            P(("seg", "rank"), None),
            P(("seg", "rank"), None),
        ),
        out_specs=(P(None, ("seg", "rank")), P(None, ("seg", "rank"))),
        check_vma=False,
    )
```

```python
import functools
import math

import jax
import jax.numpy as jnp
import ml_dtypes
import numpy as np
from jax import lax
from jax.experimental import pallas as pl
from jax.experimental.pallas import tpu as pltpu
from jax.sharding import PartitionSpec as P


def shifted(array, axis, by):
    count = lax.axis_size(axis)
    pairs = [(i, i + by) for i in range(count) if 0 <= i + by < count]
    return lax.ppermute(array, axis, pairs)


def gll_tables():
    points = np.array([-1.0, -math.sqrt(3.0 / 7.0), 0.0, math.sqrt(3.0 / 7.0), 1.0])
    weights = np.array([0.1, 49.0 / 90.0, 32.0 / 45.0, 49.0 / 90.0, 0.1])
    barycentric = np.array(
        [1.0 / np.prod([points[j] - points[m] for m in range(5) if m != j]) for j in range(5)]
    )
    slopes = np.zeros((5, 5))
    for i in range(5):
        for j in range(5):
            if i != j:
                slopes[i, j] = barycentric[j] / barycentric[i] / (points[i] - points[j])
        slopes[i, i] = -np.sum(slopes[i])

    def lagrange_at(where):
        table = np.ones((5, 5))
        for a in range(5):
            for j in range(5):
                for m in range(5):
                    if m != j:
                        table[a, j] *= (where[a] - points[m]) / (points[j] - points[m])
        return table

    def blend(value, side):
        return (1.0 - value) / 2.0 if side == 0 else (1.0 + value) / 2.0

    def flat(i, j, k):
        return i * 25 + j * 5 + k

    ends = (0, 4)
    gordon = np.zeros((125, 125))
    for i in range(5):
        for j in range(5):
            for k in range(5):
                r, s, t = (points[i], points[j], points[k])
                target = flat(i, j, k)
                for a in range(2):
                    gordon[target, flat(ends[a], j, k)] += blend(r, a)
                    gordon[target, flat(i, ends[a], k)] += blend(s, a)
                    gordon[target, flat(i, j, ends[a])] += blend(t, a)
                    for b in range(2):
                        gordon[target, flat(ends[a], ends[b], k)] -= blend(r, a) * blend(s, b)
                        gordon[target, flat(ends[a], j, ends[b])] -= blend(r, a) * blend(t, b)
                        gordon[target, flat(i, ends[a], ends[b])] -= blend(s, a) * blend(t, b)
                        for c in range(2):
                            gordon[target, flat(ends[a], ends[b], ends[c])] += (
                                blend(r, a) * blend(s, b) * blend(t, c)
                            )
    identity = np.eye(5)
    derivs = [
        np.kron(np.kron(slopes, identity), identity),
        np.kron(np.kron(identity, slopes), identity),
        np.kron(np.kron(identity, identity), slopes),
    ]
    mass_weights = np.kron(np.kron(weights, weights), weights)
    face_weights = np.kron(weights, weights)
    tangents = [(1, 2), (1, 2), (0, 2), (0, 2), (0, 1), (0, 1)]
    boundary = [
        flat(i, j, k)
        for i in range(5)
        for j in range(5)
        for k in range(5)
        if i in ends or j in ends or k in ends
    ]
    halves = [lagrange_at((points - 1.0) / 2.0), lagrange_at((points + 1.0) / 2.0)]
    steps = [
        [np.kron(np.kron(half, identity), identity) @ gordon for half in halves],
        [np.kron(np.kron(identity, half), identity) for half in halves],
        [np.kron(np.kron(identity, identity), half) for half in halves],
    ]
    nodes = []
    for side in (0, 4):
        nodes.append([flat(side, j, k) for j in range(5) for k in range(5)])
    for side in (0, 4):
        nodes.append([flat(i, side, k) for i in range(5) for k in range(5)])
    for side in (0, 4):
        nodes.append([flat(i, j, side) for i in range(5) for j in range(5)])
    corners = [flat(i, j, k) for i in ends for j in ends for k in ends]
    return (steps, derivs, mass_weights, face_weights, nodes, tangents, boundary, corners)


HELD = 104
OWNERS = 3 * HELD
WIDTH = 256
NT = (((1,), (1,)), ((), ()))
FACES = 160
STRIP = 32
SIDES = (0, 256, 512)
DERIVS = 768
EARLIER = DERIVS + 384 + 2 * FACES
PICK = EARLIER + 256


def parts_of(table):
    high = table.astype(ml_dtypes.bfloat16)
    low = (table - high.astype(np.float64)).astype(ml_dtypes.bfloat16)
    return np.concatenate([high, high, low], axis=1)


def padded(table, rows, columns):
    out = np.zeros((rows, columns))
    out[: table.shape[0], : table.shape[1]] = table
    return out


def operators():
    steps, derivs, mass_weights, face_weights, nodes, tangents, boundary, corners = gll_tables()
    pick = np.zeros((OWNERS, 375))
    for c in range(3):
        for row, node in enumerate(boundary):
            pick[c * HELD + row, c * 125 + node] += 1.0
            for corner in corners:
                pick[c * HELD + row, c * 125 + corner] -= 0.125
    first = np.concatenate([padded(step[:, boundary], 128, HELD) for step in steps[0]])
    second = np.concatenate([padded(step, 128, 128) for step in steps[1]])
    third = np.concatenate([padded(step, 128, 128) for step in steps[2]])
    rows = [padded(derivs[0] * mass_weights[:, None], 128, 128)]
    rows += [padded(derivs[d], 128, 128) for d in (1, 2)]
    along = [derivs[tangents[f][0]][nodes[f]] * face_weights[:, None] for f in range(6)]
    across = [derivs[tangents[f][1]][nodes[f]] for f in range(6)]
    for part in (along, across):
        rows += [padded(np.concatenate(part[:5]), 128, 128), padded(part[5], 32, 128)]
    earlier = np.triu(np.ones((256, 256)), 1)
    tables = [parts_of(table) for table in (first, second, third, np.concatenate(rows))] + [earlier, pick]
    tables = [padded(table.astype(np.float64), table.shape[0], 384) for table in tables]
    return pick, jnp.asarray(np.concatenate(tables).astype(ml_dtypes.bfloat16))


def stacked(values):
    high = values.astype(jnp.bfloat16)
    low = (values - high.astype(jnp.float32)).astype(jnp.bfloat16)
    return jnp.concatenate([high, low, high], axis=0)


def octant_bits(octant):
    bits = []
    for size in (4.0, 2.0, 1.0):
        bit = jnp.where(octant > size + 0.5, 1.0, 0.0)
        octant = octant - size * bit
        bits.append(jnp.concatenate([bit, bit, bit], axis=1))
    return bits


def chosen_children(block, keys, span):
    f32 = jnp.float32
    slot = lax.broadcasted_iota(jnp.int32, (span, 256), 0).astype(f32)
    hit = jnp.zeros((span, 256), f32)
    for o in range(8):
        hit = jnp.where(keys[o] == slot, float(o + 1), hit)
    high = block.astype(jnp.bfloat16).astype(f32)
    both = jnp.concatenate([high, block - high], axis=0).astype(jnp.bfloat16)
    chosen = jnp.where(hit > 0.5, 1.0, 0.0).astype(jnp.bfloat16)
    held = lax.dot_general(both, chosen, NT, preferred_element_type=f32)
    octant = lax.dot_general(
        jnp.ones((8, 256), jnp.bfloat16), hit.astype(jnp.bfloat16), NT, preferred_element_type=f32
    )
    return held, octant


def masses(held, octant, table_ref):
    f32 = jnp.float32
    bits = octant_bits(octant[0:1, :])
    high = jnp.concatenate([held[c * HELD : (c + 1) * HELD] for c in range(3)], axis=1)
    low = jnp.concatenate([held[(c + 3) * HELD : (c + 4) * HELD] for c in range(3)], axis=1)
    operand = jnp.concatenate([high, low, high], axis=0).astype(jnp.bfloat16)
    for start, bit in zip(SIDES, bits):
        table = table_ref[start : start + 256, : operand.shape[0]]
        sides = jnp.dot(table, operand, preferred_element_type=f32)
        operand = stacked(jnp.where(bit > 0.5, sides[128:], sides[:128]))

    def components(start, rows):
        table = table_ref[DERIVS + start : DERIVS + start + rows, :]
        values = jnp.dot(table, operand, preferred_element_type=f32)
        return [values[:, c * WIDTH : (c + 1) * WIDTH] for c in range(3)]

    def crossed(p, q):
        return [p[1] * q[2] - p[2] * q[1], p[2] * q[0] - p[0] * q[2], p[0] * q[1] - p[1] * q[0]]

    first, second, third = (components(128 * d, 128) for d in range(3))
    normal = crossed(second, third)
    mass = (first[0] * normal[0] + first[1] * normal[1] + first[2] * normal[2])[:125]
    normal = crossed(components(384, FACES), components(384 + FACES, FACES))
    face = jnp.sqrt(normal[0] * normal[0] + normal[1] * normal[1] + normal[2] * normal[2])
    return mass, face


def keys_of(mask, earlier):
    before = jnp.dot(mask.astype(jnp.bfloat16), earlier, preferred_element_type=jnp.float32)
    total = jnp.sum(before, axis=0, keepdims=True)
    keys = []
    for o in range(8):
        row = mask[o : o + 1, :]
        keys.append(jnp.where(row > 0.5, total, -1e6))
        total = total + row
    return keys


def geometry_kernel(cap, block_ref, mask_ref, table_ref, mass_ref, face_ref):
    gathered, octants = [], []
    aligned = cap % 128 == 0
    for s in range(WIDTH // cap):
        keys = keys_of(mask_ref[s], table_ref[EARLIER : EARLIER + 256, :256])
        if not aligned:
            keys = [key + float(s * cap) for key in keys]
        held, octant = chosen_children(block_ref[s, :OWNERS, :], keys, cap if aligned else WIDTH)
        gathered.append(held)
        octants.append(octant)
    if aligned:
        held = jnp.concatenate(gathered, axis=1)
        octant = jnp.concatenate(octants, axis=1)
    else:
        held = sum(gathered[1:], gathered[0])
        octant = sum(octants[1:], octants[0])
    mass, face = masses(held, octant, table_ref)
    mass_ref[...] = mass
    face_ref[...] = face


def whole_spec(array):
    return pl.BlockSpec(array.shape, lambda i: (0,) * array.ndim)


def geometry(blocks, mask, tables, cap):
    devices = blocks.shape[0]
    slots = devices * cap
    group = WIDTH // cap
    return pl.pallas_call(
        lambda *refs: geometry_kernel(cap, *refs),
        grid=(slots // WIDTH,),
        in_specs=[
            pl.BlockSpec((group,) + blocks.shape[1:], lambda i: (i, 0, 0)),
            pl.BlockSpec((group,) + mask.shape[1:], lambda i: (i, 0, 0)),
            whole_spec(tables),
        ],
        out_specs=[
            pl.BlockSpec((125, WIDTH), lambda i: (0, i)),
            pl.BlockSpec((FACES, WIDTH), lambda i: (0, i)),
        ],
        out_shape=[
            jax.ShapeDtypeStruct((125, slots), jnp.float32),
            jax.ShapeDtypeStruct((FACES, slots), jnp.float32),
        ],
        compiler_params=pltpu.CompilerParams(vmem_limit_bytes=48 * 1024 * 1024),
        name="geometry",
    )(blocks, mask, tables)


def picked_coords(nodes, marks, pick):
    f32 = jnp.float32
    row = lax.broadcasted_iota(jnp.int32, (nodes.shape[1], marks.shape[1]), 0)
    chosen = jnp.where(row == marks, 1.0, 0.0).astype(jnp.bfloat16)
    coords = None
    for _ in range(3):
        part = nodes.astype(jnp.bfloat16)
        nodes = nodes - part.astype(f32)
        part = jnp.dot(part, chosen, preferred_element_type=f32).astype(jnp.bfloat16)
        part = jnp.dot(pick, part, preferred_element_type=f32)
        coords = part if coords is None else coords + part
    return coords


MESH = pl.DeviceIdType.MESH
DELAY = 5
CHIP_Z = 4


def gather_kernel(
    nodes_ref, marks_ref, owners_ref, table_ref,
    mass_ref, face_ref, low_ref, before_ref, after_ref, held_ref,
    send_up, send_down, send_x, send_y, send_dx, send_dy, send_c, send_next, send_prev, send_low_next, send_low_prev,
    recv_z, recv_x, recv_y, recv_dx, recv_dy, recv_c, recv_before, recv_after, recv_low_before, recv_low_after,
):
    s = lax.axis_index("seg")
    rank = lax.axis_index("rank")
    z, core = rank // 2, rank % 2
    me = s * (2 * CHIP_Z) + rank
    half = held_ref.shape[1] // 2
    sx = s + 1 - 2 * (s % 2)
    sy = s + 2 - 4 * (s // 2)
    sd = sx + sy - s
    at_x, at_y, at_c = (sx, rank), (sy, rank), (s, rank + 1 - 2 * core)
    above, below = (s, rank + 2), (s, rank - 2)
    next_one, prev_one = (s, rank + 1), (s, rank - 1)
    has_above, has_below = z < CHIP_Z - 1, z > 0
    has_next, has_prev = rank < 2 * CHIP_Z - 1, rank > 0
    step_away = (core == 1) & has_next | (core == 0) & has_prev
    away = (s, rank + 2 * core - 1)

    def number(seg, level):
        return (seg * CHIP_Z + level) * 2 + core

    def level_of(j):
        low = z // 2
        near = jnp.where(j == 0, z, z + 1 - 2 * (z % 2))
        far = jnp.where(low == 0, j, 3 - j)
        return jnp.where(j < 2, near, far)

    def remote(src, dst, send, recv, target):
        return pltpu.make_async_remote_copy(
            src_ref=src, dst_ref=dst, send_sem=send, recv_sem=recv, device_id=target, device_id_type=MESH
        )

    def whole(seg, level, send, recv, target):
        place = held_ref.at[number(seg, level)]
        return remote(place, place, send, recv, target)

    def up(level):
        return whole(s, level, send_up.at[level], recv_z.at[level], above)

    def down(level):
        return whole(s, level, send_down.at[level], recv_z.at[level], below)

    def to_x(level):
        return whole(s, level, send_x.at[level], recv_x.at[level], at_x)

    def to_y(level):
        return whole(s, level, send_y.at[level], recv_y.at[level], at_y)

    def half_to_y(level):
        place = held_ref.at[number(sx, level), pl.ds(0, half)]
        return remote(place, place, send_dy.at[level], recv_dy.at[level], at_y)

    def half_to_x(level):
        place = held_ref.at[number(sy, level), pl.ds(half, half)]
        return remote(place, place, send_dx.at[level], recv_dx.at[level], at_x)

    def to_core(seg, level):
        chip = seg * CHIP_Z + level
        return whole(seg, level, send_c.at[chip], recv_c.at[chip], at_c)

    def from_core(chip):
        place = held_ref.at[chip * 2 + 1 - core]
        return remote(place, place, send_c.at[chip], recv_c.at[chip], at_c)

    def from_x(level):
        return whole(sx, level, send_x.at[level], recv_x.at[level], at_x)

    def from_y(level):
        return whole(sy, level, send_y.at[level], recv_y.at[level], at_y)

    def half_from_y(level):
        place = held_ref.at[number(sd, level), pl.ds(0, half)]
        return remote(place, place, send_dy.at[level], recv_dy.at[level], at_y)

    def half_from_x(level):
        place = held_ref.at[number(sd, level), pl.ds(half, half)]
        return remote(place, place, send_dx.at[level], recv_dx.at[level], at_x)

    slots = face_ref.shape[1]

    def strip(ref, chip):
        rows = pl.ds(ref.shape[0] - STRIP, STRIP)
        return ref.at[rows, pl.ds(pl.multiple_of(chip * WIDTH, WIDTH), WIDTH)]

    def part(number, chip):
        return low_ref.at[pl.ds(pl.multiple_of(number * slots + chip * WIDTH, WIDTH), WIDTH)]

    def to_next(chip):
        return [
            remote(
                strip(face_ref, chip), strip(before_ref, chip), send_next.at[chip], recv_before.at[chip], next_one
            ),
            remote(
                part(1, chip), part(0, chip), send_low_next.at[chip], recv_low_before.at[chip], next_one
            ),
        ]

    def to_prev(chip):
        return [
            remote(
                strip(face_ref, chip), strip(after_ref, chip), send_prev.at[chip], recv_after.at[chip], prev_one
            ),
            remote(
                part(1, chip), part(2, chip), send_low_prev.at[chip], recv_low_after.at[chip], prev_one
            ),
        ]

    def from_prev(chip):
        return [
            remote(
                strip(face_ref, chip), strip(before_ref, chip), send_prev.at[chip], recv_before.at[chip], prev_one
            ),
            remote(
                part(1, chip), part(0, chip), send_low_prev.at[chip], recv_low_before.at[chip], prev_one
            ),
        ]

    def from_next(chip):
        return [
            remote(
                strip(face_ref, chip), strip(after_ref, chip), send_next.at[chip], recv_after.at[chip], next_one
            ),
            remote(
                part(1, chip), part(2, chip), send_low_next.at[chip], recv_low_after.at[chip], next_one
            ),
        ]

    def send_faces(chip):
        @pl.when(has_next)
        def _():
            for copy in to_next(chip):
                copy.start()

        @pl.when(has_prev)
        def _():
            for copy in to_prev(chip):
                copy.start()

    barrier = pltpu.get_barrier_semaphore()

    def greet(target):
        pl.semaphore_signal(barrier, inc=1, device_id=target, device_id_type=MESH)

    for target in (at_x, at_y, at_c):
        greet(target)
    for present, target in ((has_above, above), (has_below, below), (step_away, away)):
        pl.when(present)(functools.partial(greet, target))
    held_ref[me, :OWNERS, :] = picked_coords(nodes_ref[...], marks_ref[...], table_ref[PICK : PICK + OWNERS, :375])
    held_ref[me, OWNERS:, :] = owners_ref[...]
    peers = 3 + sum(present.astype(jnp.int32) for present in (has_above, has_below, step_away))
    pl.semaphore_wait(barrier, peers)

    def spread(level):
        pl.when(has_above & (level <= z))(lambda: up(level).start())
        pl.when(has_below & (level >= z))(lambda: down(level).start())
        to_x(level).start()
        to_y(level).start()
        to_core(s, level).start()

    spread(z)

    @pl.when(rank == 0)
    def _():
        before_ref[...] = jnp.zeros_like(before_ref)
        low_ref[:slots, :] = jnp.zeros((slots, 128), jnp.float32)

    @pl.when(rank == 2 * CHIP_Z - 1)
    def _():
        after_ref[...] = jnp.zeros_like(after_ref)
        low_ref[2 * slots :, :] = jnp.zeros((slots, 128), jnp.float32)

    own = me.astype(jnp.float32)

    def along_z(position):
        level = level_of(position)
        whole(s, level, send_up.at[level], recv_z.at[level], at_c).wait_recv()
        spread(level)

    def diagonal(level):
        half_from_x(level).wait_recv()
        half_from_y(level).wait_recv()
        to_core(sd, level).start()

    middle = (has_above & has_below).astype(jnp.int32)

    def step_of(t):
        j, k = (t + 3) // 4 - 1, (t + 3) % 4
        column = (k == 0) & (j < CHIP_Z - 1) | (t == 0)
        slanted = (k == 3) & (j >= 1) | (t == 4 * CHIP_Z + 1)
        position = jnp.where(t == 0, 0, jnp.where(column, j + 1, jnp.where(slanted, j - 1, j)))
        seg = jnp.where(column, s, jnp.where(slanted, sd, jnp.where(k == 1, sx, sy)))
        return column | slanted | (k == 1) | (k == 2), seg * CHIP_Z + level_of(position)

    @pl.loop(0, 4 * CHIP_Z + 2)
    def _(t):
        j, k = (t + 3) // 4 - 1, (t + 3) % 4

        @pl.when((k == 0) & (j >= 0) & (j < CHIP_Z))
        def _():
            pl.when((middle == 1) & (j == 0))(lambda: along_z(1))
            pl.when(j + 1 + middle < CHIP_Z)(lambda: along_z(j + 1 + middle))
            level = level_of(j)
            from_x(level).wait_recv()
            half_to_y(level).start()
            to_core(sx, level).start()
            from_y(level).wait_recv()
            half_to_x(level).start()
            to_core(sy, level).start()

        pl.when((k == 2) & (j >= 1) & (j < CHIP_Z))(lambda: diagonal(level_of(j - 1)))
        pl.when(t == 4 * CHIP_Z + 1)(lambda: diagonal(level_of(CHIP_Z - 1)))
        active, chip = step_of(t)

        @pl.when(active)
        def _():
            from_core(chip).wait_recv()
            gathered, octants = [], []
            for c in range(2):
                block = held_ref[chip * 2 + c]
                mask = jnp.where(block[OWNERS:, :] == own, 1.0, 0.0)
                held, octant = chosen_children(block[:OWNERS, :], keys_of(mask, table_ref[EARLIER : EARLIER + 256, :256]), WIDTH // 2)
                gathered.append(held)
                octants.append(octant)
            mass, face = masses(
                jnp.concatenate(gathered, axis=1), jnp.concatenate(octants, axis=1), table_ref
            )
            lanes = pl.ds(pl.multiple_of(chip * WIDTH, WIDTH), WIDTH)
            mass_ref[:, lanes] = mass
            face_ref[:, lanes] = face
            low_ref[pl.ds(pl.multiple_of(slots + chip * WIDTH, WIDTH), WIDTH), :] = face[:128].T
            pl.when(t >= DELAY)(lambda: send_faces(chip))

        waiting, old = step_of(jnp.maximum(t - DELAY, 0))
        pl.when((t >= DELAY) & (t < 2 * DELAY) & waiting)(lambda: send_faces(old))

    @pl.loop(0, CHIP_Z)
    def _(level):
        pl.when(has_above & (level <= z))(lambda: up(level).wait_send())
        pl.when(has_below & (level >= z))(lambda: down(level).wait_send())
        to_x(level).wait_send()
        to_y(level).wait_send()
        half_to_x(level).wait_send()
        half_to_y(level).wait_send()

    @pl.loop(0, 4 * CHIP_Z)
    def _(chip):
        to_core(chip // CHIP_Z, chip % CHIP_Z).wait_send()

        @pl.when(has_next)
        def _():
            for copy in to_next(chip):
                copy.wait_send()
            for copy in from_next(chip):
                copy.wait_recv()

        @pl.when(has_prev)
        def _():
            for copy in to_prev(chip):
                copy.wait_send()
            for copy in from_prev(chip):
                copy.wait_recv()


def gather_and_compute(nodes, marks, owners, tables, cap):
    devices = 8 * CHIP_Z
    slots = devices * cap
    vmem = pl.BlockSpec(memory_space=pltpu.VMEM)
    faces = jax.ShapeDtypeStruct((FACES, slots), jnp.float32)
    low = jax.ShapeDtypeStruct((3 * slots, 128), jnp.float32)
    strips = jax.ShapeDtypeStruct((STRIP, slots), jnp.float32)
    dma = pltpu.SemaphoreType.DMA
    chips = 4 * CHIP_Z
    return pl.pallas_call(
        gather_kernel,
        in_specs=[vmem] * 4,
        out_specs=[vmem] * 5,
        out_shape=[jax.ShapeDtypeStruct((125, slots), jnp.float32), faces, low, strips, strips],
        scratch_shapes=[pltpu.VMEM((devices, OWNERS + 8, owners.shape[1]), jnp.float32)]
        + [dma((CHIP_Z,))] * 6
        + [dma((chips,))] * 5
        + [dma((CHIP_Z,))] * 5
        + [dma((chips,))] * 5,
        compiler_params=pltpu.CompilerParams(
            collective_id=0, has_side_effects=True, vmem_limit_bytes=48 * 1024 * 1024
        ),
        name="gather_and_compute",
    )(nodes, marks, owners, tables)


def assemble_kernel(link_ref, low_ref, before_ref, own_ref, after_ref, out_ref, high_ref, row_low, row_high):
    slots = own_ref.shape[1]
    for part, ref in enumerate((before_ref, own_ref, after_ref)):

        @pl.loop(0, slots // 512)
        def _(number):
            for k in range(4):
                start = pl.multiple_of(number * 512 + k * 128, 128)
                rows = pl.ds(pl.multiple_of(part * slots + number * 512 + k * 128, 128), 128)
                high_ref[rows, :STRIP] = ref[ref.shape[0] - STRIP :, pl.ds(start, 128)].T

    lane = lax.broadcasted_iota(jnp.int32, (1, 128), 1)
    under = [lane < 25 * (g + 1) for g in range(4)]

    @pl.loop(0, slots // 128)
    def _(number):
        start = pl.multiple_of(number * 128, 128)

        @pl.loop(0, 128, step=16)
        def _(inner):
            for k in range(16):
                u = start + inner + k
                row = [link_ref[f * slots + u] for f in range(6)]
                value = low_ref[pl.ds(row[5], 1), :]
                for g in (3, 2, 1, 0):
                    value = jnp.where(under[g], low_ref[pl.ds(row[g ^ 1], 1), :], value)
                row_low[pl.ds(inner + k, 1), :] = value
                row_high[pl.ds(inner + k, 1), :] = high_ref[pl.ds(row[4], 1), :]

        low = row_low[...].T
        high = row_high[:, :STRIP].T
        fetched = [low[25 * (f ^ 1) : 25 * (f ^ 1) + 25] for f in range(4)]
        fetched += [high[0:25], low[100:125]]
        lanes = pl.ds(start, 128)
        own = [own_ref[0:125, lanes], own_ref[128:153, lanes]]
        out_ref[:, lanes] = jnp.concatenate(own, axis=0) + jnp.concatenate(fetched, axis=0)


def assemble(link, low, before, own, after):
    slots = own.shape[1]
    vmem = pl.BlockSpec(memory_space=pltpu.VMEM)
    return pl.pallas_call(
        assemble_kernel,
        in_specs=[pl.BlockSpec(memory_space=pltpu.SMEM), vmem, vmem, vmem, vmem],
        out_specs=vmem,
        out_shape=jax.ShapeDtypeStruct((150, slots), jnp.float32),
        scratch_shapes=[
            pltpu.VMEM((3 * slots, 128), jnp.float32),
            pltpu.VMEM((128, 128), jnp.float32),
            pltpu.VMEM((128, 128), jnp.float32),
        ],
        compiler_params=pltpu.CompilerParams(vmem_limit_bytes=48 * 1024 * 1024),
        name="assemble",
    )(link, low, before, own, after)


def body(parent_nodes, marks, child_owner, face_link):
    pick, tables = operators()
    devices = lax.axis_size("seg") * lax.axis_size("rank")
    me = lax.axis_index("seg") * lax.axis_size("rank") + lax.axis_index("rank")
    kids = child_owner.shape[0]
    cap = max(2, 2 * kids // devices)
    owners = child_owner.reshape(kids // 8, 8).T.astype(jnp.float32)
    if lax.axis_size("seg") == 4 and lax.axis_size("rank") == 2 * CHIP_Z and 2 * cap == WIDTH:
        mass, faces, low, before, after = gather_and_compute(parent_nodes.T, marks, owners, tables, cap)
    else:
        coords = lax.dot_general(
            jnp.asarray(pick, jnp.float32),
            parent_nodes[marks[0]],
            NT,
            precision=lax.Precision.HIGHEST,
            preferred_element_type=jnp.float32,
        )
        blocks = lax.all_gather(jnp.concatenate([coords, owners], axis=0), ("seg", "rank"))
        mask = (blocks[:, OWNERS:, :] == me.astype(jnp.float32)).astype(jnp.float32)
        mass, faces = geometry(blocks, mask, tables, cap)
        before = shifted(faces, "rank", 1)
        after = shifted(faces, "rank", -1)
        low = jnp.concatenate([before[:128].T, faces[:128].T, after[:128].T], axis=0)
        before, after = before[128:], after[128:]
    return (mass, assemble(face_link.T.reshape(-1), low, before, faces, after))


def solution(mesh):
    return jax.shard_map(
        body,
        mesh=mesh,
        in_specs=(
            P(("seg", "rank"), None),
            P(("seg", "rank"), None),
            P(("seg", "rank"), None),
            P(("seg", "rank"), None),
        ),
        out_specs=(P(None, ("seg", "rank")), P(None, ("seg", "rank"))),
        check_vma=False,
    )
```

```python
import functools
import math

import jax
import jax.numpy as jnp
import ml_dtypes
import numpy as np
from jax import lax
from jax.experimental import pallas as pl
from jax.experimental.pallas import tpu as pltpu
from jax.sharding import PartitionSpec as P


def shifted(array, axis, by):
    count = lax.axis_size(axis)
    pairs = [(i, i + by) for i in range(count) if 0 <= i + by < count]
    return lax.ppermute(array, axis, pairs)


def gll_tables():
    points = np.array([-1.0, -math.sqrt(3.0 / 7.0), 0.0, math.sqrt(3.0 / 7.0), 1.0])
    weights = np.array([0.1, 49.0 / 90.0, 32.0 / 45.0, 49.0 / 90.0, 0.1])
    barycentric = np.array(
        [1.0 / np.prod([points[j] - points[m] for m in range(5) if m != j]) for j in range(5)]
    )
    slopes = np.zeros((5, 5))
    for i in range(5):
        for j in range(5):
            if i != j:
                slopes[i, j] = barycentric[j] / barycentric[i] / (points[i] - points[j])
        slopes[i, i] = -np.sum(slopes[i])

    def lagrange_at(where):
        table = np.ones((5, 5))
        for a in range(5):
            for j in range(5):
                for m in range(5):
                    if m != j:
                        table[a, j] *= (where[a] - points[m]) / (points[j] - points[m])
        return table

    def blend(value, side):
        return (1.0 - value) / 2.0 if side == 0 else (1.0 + value) / 2.0

    def flat(i, j, k):
        return i * 25 + j * 5 + k

    ends = (0, 4)
    gordon = np.zeros((125, 125))
    for i in range(5):
        for j in range(5):
            for k in range(5):
                r, s, t = (points[i], points[j], points[k])
                target = flat(i, j, k)
                for a in range(2):
                    gordon[target, flat(ends[a], j, k)] += blend(r, a)
                    gordon[target, flat(i, ends[a], k)] += blend(s, a)
                    gordon[target, flat(i, j, ends[a])] += blend(t, a)
                    for b in range(2):
                        gordon[target, flat(ends[a], ends[b], k)] -= blend(r, a) * blend(s, b)
                        gordon[target, flat(ends[a], j, ends[b])] -= blend(r, a) * blend(t, b)
                        gordon[target, flat(i, ends[a], ends[b])] -= blend(s, a) * blend(t, b)
                        for c in range(2):
                            gordon[target, flat(ends[a], ends[b], ends[c])] += (
                                blend(r, a) * blend(s, b) * blend(t, c)
                            )
    identity = np.eye(5)
    derivs = [
        np.kron(np.kron(slopes, identity), identity),
        np.kron(np.kron(identity, slopes), identity),
        np.kron(np.kron(identity, identity), slopes),
    ]
    mass_weights = np.kron(np.kron(weights, weights), weights)
    face_weights = np.kron(weights, weights)
    tangents = [(1, 2), (1, 2), (0, 2), (0, 2), (0, 1), (0, 1)]
    boundary = [
        flat(i, j, k)
        for i in range(5)
        for j in range(5)
        for k in range(5)
        if i in ends or j in ends or k in ends
    ]
    halves = [lagrange_at((points - 1.0) / 2.0), lagrange_at((points + 1.0) / 2.0)]
    steps = [
        [np.kron(np.kron(half, identity), identity) @ gordon for half in halves],
        [np.kron(np.kron(identity, half), identity) for half in halves],
        [np.kron(np.kron(identity, identity), half) for half in halves],
    ]
    nodes = []
    for side in (0, 4):
        nodes.append([flat(side, j, k) for j in range(5) for k in range(5)])
    for side in (0, 4):
        nodes.append([flat(i, side, k) for i in range(5) for k in range(5)])
    for side in (0, 4):
        nodes.append([flat(i, j, side) for i in range(5) for j in range(5)])
    corners = [flat(i, j, k) for i in ends for j in ends for k in ends]
    return (steps, derivs, mass_weights, face_weights, nodes, tangents, boundary, corners)


HELD = 104
OWNERS = 3 * HELD
WIDTH = 256
NT = (((1,), (1,)), ((), ()))
FACES = 160
STRIP = 32
SIDES = (0, 256, 512)
DERIVS = 768
EARLIER = DERIVS + 384 + 2 * FACES
PICK = EARLIER + 256


def parts_of(table):
    high = table.astype(ml_dtypes.bfloat16)
    low = (table - high.astype(np.float64)).astype(ml_dtypes.bfloat16)
    return np.concatenate([high, high, low], axis=1)


def padded(table, rows, columns):
    out = np.zeros((rows, columns))
    out[: table.shape[0], : table.shape[1]] = table
    return out


def operators():
    steps, derivs, mass_weights, face_weights, nodes, tangents, boundary, corners = gll_tables()
    pick = np.zeros((OWNERS, 375))
    for c in range(3):
        for row, node in enumerate(boundary):
            pick[c * HELD + row, c * 125 + node] += 1.0
            for corner in corners:
                pick[c * HELD + row, c * 125 + corner] -= 0.125
    first = np.concatenate([padded(step[:, boundary], 128, HELD) for step in steps[0]])
    second = np.concatenate([padded(step, 128, 128) for step in steps[1]])
    third = np.concatenate([padded(step, 128, 128) for step in steps[2]])
    rows = [padded(derivs[0] * mass_weights[:, None], 128, 128)]
    rows += [padded(derivs[d], 128, 128) for d in (1, 2)]
    along = [derivs[tangents[f][0]][nodes[f]] * face_weights[:, None] for f in range(6)]
    across = [derivs[tangents[f][1]][nodes[f]] for f in range(6)]
    for part in (along, across):
        rows += [padded(np.concatenate(part[:5]), 128, 128), padded(part[5], 32, 128)]
    earlier = np.triu(np.ones((256, 256)), 1)
    tables = [parts_of(table) for table in (first, second, third, np.concatenate(rows))] + [earlier, pick]
    tables = [padded(table.astype(np.float64), table.shape[0], 384) for table in tables]
    return pick, jnp.asarray(np.concatenate(tables).astype(ml_dtypes.bfloat16))


def stacked(values):
    high = values.astype(jnp.bfloat16)
    low = (values - high.astype(jnp.float32)).astype(jnp.bfloat16)
    return jnp.concatenate([high, low, high], axis=0)


def octant_bits(octant):
    bits = []
    for size in (4.0, 2.0, 1.0):
        bit = jnp.where(octant > size + 0.5, 1.0, 0.0)
        octant = octant - size * bit
        bits.append(jnp.concatenate([bit, bit, bit], axis=1))
    return bits


def chosen_children(block, keys, span):
    f32 = jnp.float32
    slot = lax.broadcasted_iota(jnp.int32, (span, 256), 0).astype(f32)
    hit = jnp.zeros((span, 256), f32)
    for o in range(8):
        hit = jnp.where(keys[o] == slot, float(o + 1), hit)
    high = block.astype(jnp.bfloat16).astype(f32)
    both = jnp.concatenate([high, block - high], axis=0).astype(jnp.bfloat16)
    chosen = jnp.where(hit > 0.5, 1.0, 0.0).astype(jnp.bfloat16)
    held = lax.dot_general(both, chosen, NT, preferred_element_type=f32)
    octant = lax.dot_general(
        jnp.ones((8, 256), jnp.bfloat16), hit.astype(jnp.bfloat16), NT, preferred_element_type=f32
    )
    return held, octant


def masses(held, octant, table_ref):
    f32 = jnp.float32
    bits = octant_bits(octant[0:1, :])
    high = jnp.concatenate([held[c * HELD : (c + 1) * HELD] for c in range(3)], axis=1)
    low = jnp.concatenate([held[(c + 3) * HELD : (c + 4) * HELD] for c in range(3)], axis=1)
    operand = jnp.concatenate([high, low, high], axis=0).astype(jnp.bfloat16)
    for start, bit in zip(SIDES, bits):
        table = table_ref[start : start + 256, : operand.shape[0]]
        sides = jnp.dot(table, operand, preferred_element_type=f32)
        operand = stacked(jnp.where(bit > 0.5, sides[128:], sides[:128]))

    def components(start, rows):
        table = table_ref[DERIVS + start : DERIVS + start + rows, :]
        values = jnp.dot(table, operand, preferred_element_type=f32)
        return [values[:, c * WIDTH : (c + 1) * WIDTH] for c in range(3)]

    def crossed(p, q):
        return [p[1] * q[2] - p[2] * q[1], p[2] * q[0] - p[0] * q[2], p[0] * q[1] - p[1] * q[0]]

    first, second, third = (components(128 * d, 128) for d in range(3))
    normal = crossed(second, third)
    mass = (first[0] * normal[0] + first[1] * normal[1] + first[2] * normal[2])[:125]
    normal = crossed(components(384, FACES), components(384 + FACES, FACES))
    face = jnp.sqrt(normal[0] * normal[0] + normal[1] * normal[1] + normal[2] * normal[2])
    return mass, face


def keys_of(mask, earlier):
    before = jnp.dot(mask.astype(jnp.bfloat16), earlier, preferred_element_type=jnp.float32)
    total = jnp.sum(before, axis=0, keepdims=True)
    keys = []
    for o in range(8):
        row = mask[o : o + 1, :]
        keys.append(jnp.where(row > 0.5, total, -1e6))
        total = total + row
    return keys


def geometry_kernel(cap, block_ref, mask_ref, table_ref, mass_ref, face_ref):
    gathered, octants = [], []
    aligned = cap % 128 == 0
    for s in range(WIDTH // cap):
        keys = keys_of(mask_ref[s], table_ref[EARLIER : EARLIER + 256, :256])
        if not aligned:
            keys = [key + float(s * cap) for key in keys]
        held, octant = chosen_children(block_ref[s, :OWNERS, :], keys, cap if aligned else WIDTH)
        gathered.append(held)
        octants.append(octant)
    if aligned:
        held = jnp.concatenate(gathered, axis=1)
        octant = jnp.concatenate(octants, axis=1)
    else:
        held = sum(gathered[1:], gathered[0])
        octant = sum(octants[1:], octants[0])
    mass, face = masses(held, octant, table_ref)
    mass_ref[...] = mass
    face_ref[...] = face


def whole_spec(array):
    return pl.BlockSpec(array.shape, lambda i: (0,) * array.ndim)


def geometry(blocks, mask, tables, cap):
    devices = blocks.shape[0]
    slots = devices * cap
    group = WIDTH // cap
    return pl.pallas_call(
        lambda *refs: geometry_kernel(cap, *refs),
        grid=(slots // WIDTH,),
        in_specs=[
            pl.BlockSpec((group,) + blocks.shape[1:], lambda i: (i, 0, 0)),
            pl.BlockSpec((group,) + mask.shape[1:], lambda i: (i, 0, 0)),
            whole_spec(tables),
        ],
        out_specs=[
            pl.BlockSpec((125, WIDTH), lambda i: (0, i)),
            pl.BlockSpec((FACES, WIDTH), lambda i: (0, i)),
        ],
        out_shape=[
            jax.ShapeDtypeStruct((125, slots), jnp.float32),
            jax.ShapeDtypeStruct((FACES, slots), jnp.float32),
        ],
        compiler_params=pltpu.CompilerParams(vmem_limit_bytes=48 * 1024 * 1024),
        name="geometry",
    )(blocks, mask, tables)


def picked_coords(nodes, marks, pick):
    f32 = jnp.float32
    row = lax.broadcasted_iota(jnp.int32, (nodes.shape[1], marks.shape[1]), 0)
    chosen = jnp.where(row == marks, 1.0, 0.0).astype(jnp.bfloat16)
    coords = None
    for _ in range(3):
        part = nodes.astype(jnp.bfloat16)
        nodes = nodes - part.astype(f32)
        part = jnp.dot(part, chosen, preferred_element_type=f32).astype(jnp.bfloat16)
        part = jnp.dot(pick, part, preferred_element_type=f32)
        coords = part if coords is None else coords + part
    return coords


MESH = pl.DeviceIdType.MESH
DELAY = 2
CHIP_Z = 4


def gather_kernel(
    nodes_ref, marks_ref, owners_ref, table_ref,
    mass_ref, face_ref, low_ref, before_ref, after_ref, held_ref,
    send_up, send_down, send_x, send_y, send_dx, send_dy, send_c, send_next, send_prev, send_low_next, send_low_prev,
    recv_z, recv_x, recv_y, recv_dx, recv_dy, recv_c, recv_before, recv_after, recv_low_before, recv_low_after,
):
    s = lax.axis_index("seg")
    rank = lax.axis_index("rank")
    z, core = rank // 2, rank % 2
    me = s * (2 * CHIP_Z) + rank
    half = held_ref.shape[1] // 2
    sx = s + 1 - 2 * (s % 2)
    sy = s + 2 - 4 * (s // 2)
    sd = sx + sy - s
    at_x, at_y, at_c = (sx, rank), (sy, rank), (s, rank + 1 - 2 * core)
    above, below = (s, rank + 2), (s, rank - 2)
    next_one, prev_one = (s, rank + 1), (s, rank - 1)
    has_above, has_below = z < CHIP_Z - 1, z > 0
    has_next, has_prev = rank < 2 * CHIP_Z - 1, rank > 0
    step_away = (core == 1) & has_next | (core == 0) & has_prev
    away = (s, rank + 2 * core - 1)

    def number(seg, level):
        return (seg * CHIP_Z + level) * 2 + core

    def level_of(j):
        low = z // 2
        near = jnp.where(j == 0, z, z + 1 - 2 * (z % 2))
        far = jnp.where(low == 0, j, 3 - j)
        return jnp.where(j < 2, near, far)

    def remote(src, dst, send, recv, target):
        return pltpu.make_async_remote_copy(
            src_ref=src, dst_ref=dst, send_sem=send, recv_sem=recv, device_id=target, device_id_type=MESH
        )

    def whole(seg, level, send, recv, target):
        place = held_ref.at[number(seg, level)]
        return remote(place, place, send, recv, target)

    def up(level):
        return whole(s, level, send_up.at[level], recv_z.at[level], above)

    def down(level):
        return whole(s, level, send_down.at[level], recv_z.at[level], below)

    def to_x(level):
        return whole(s, level, send_x.at[level], recv_x.at[level], at_x)

    def to_y(level):
        return whole(s, level, send_y.at[level], recv_y.at[level], at_y)

    def half_to_y(level):
        place = held_ref.at[number(sx, level), pl.ds(0, half)]
        return remote(place, place, send_dy.at[level], recv_dy.at[level], at_y)

    def half_to_x(level):
        place = held_ref.at[number(sy, level), pl.ds(half, half)]
        return remote(place, place, send_dx.at[level], recv_dx.at[level], at_x)

    def to_core(seg, level):
        chip = seg * CHIP_Z + level
        return whole(seg, level, send_c.at[chip], recv_c.at[chip], at_c)

    def from_core(chip):
        place = held_ref.at[chip * 2 + 1 - core]
        return remote(place, place, send_c.at[chip], recv_c.at[chip], at_c)

    def from_x(level):
        return whole(sx, level, send_x.at[level], recv_x.at[level], at_x)

    def from_y(level):
        return whole(sy, level, send_y.at[level], recv_y.at[level], at_y)

    def half_from_y(level):
        place = held_ref.at[number(sd, level), pl.ds(0, half)]
        return remote(place, place, send_dy.at[level], recv_dy.at[level], at_y)

    def half_from_x(level):
        place = held_ref.at[number(sd, level), pl.ds(half, half)]
        return remote(place, place, send_dx.at[level], recv_dx.at[level], at_x)

    slots = face_ref.shape[1]

    def strip(ref, chip):
        rows = pl.ds(ref.shape[0] - STRIP, STRIP)
        return ref.at[rows, pl.ds(pl.multiple_of(chip * WIDTH, WIDTH), WIDTH)]

    def part(number, chip):
        return low_ref.at[pl.ds(pl.multiple_of(number * slots + chip * WIDTH, WIDTH), WIDTH)]

    def to_next(chip):
        return [
            remote(
                strip(face_ref, chip), strip(before_ref, chip), send_next.at[chip], recv_before.at[chip], next_one
            ),
            remote(
                part(1, chip), part(0, chip), send_low_next.at[chip], recv_low_before.at[chip], next_one
            ),
        ]

    def to_prev(chip):
        return [
            remote(
                strip(face_ref, chip), strip(after_ref, chip), send_prev.at[chip], recv_after.at[chip], prev_one
            ),
            remote(
                part(1, chip), part(2, chip), send_low_prev.at[chip], recv_low_after.at[chip], prev_one
            ),
        ]

    def from_prev(chip):
        return [
            remote(
                strip(face_ref, chip), strip(before_ref, chip), send_prev.at[chip], recv_before.at[chip], prev_one
            ),
            remote(
                part(1, chip), part(0, chip), send_low_prev.at[chip], recv_low_before.at[chip], prev_one
            ),
        ]

    def from_next(chip):
        return [
            remote(
                strip(face_ref, chip), strip(after_ref, chip), send_next.at[chip], recv_after.at[chip], next_one
            ),
            remote(
                part(1, chip), part(2, chip), send_low_next.at[chip], recv_low_after.at[chip], next_one
            ),
        ]

    def send_faces(chip):
        @pl.when(has_next)
        def _():
            for copy in to_next(chip):
                copy.start()

        @pl.when(has_prev)
        def _():
            for copy in to_prev(chip):
                copy.start()

    barrier = pltpu.get_barrier_semaphore()

    def greet(target):
        pl.semaphore_signal(barrier, inc=1, device_id=target, device_id_type=MESH)

    for target in (at_x, at_y, at_c):
        greet(target)
    for present, target in ((has_above, above), (has_below, below), (step_away, away)):
        pl.when(present)(functools.partial(greet, target))
    held_ref[me, :OWNERS, :] = picked_coords(nodes_ref[...], marks_ref[...], table_ref[PICK : PICK + OWNERS, :375])
    held_ref[me, OWNERS:, :] = owners_ref[...]
    peers = 3 + sum(present.astype(jnp.int32) for present in (has_above, has_below, step_away))
    pl.semaphore_wait(barrier, peers)

    def spread(level):
        pl.when(has_above & (level <= z))(lambda: up(level).start())
        pl.when(has_below & (level >= z))(lambda: down(level).start())
        to_x(level).start()
        to_y(level).start()
        to_core(s, level).start()

    spread(z)

    @pl.when(rank == 0)
    def _():
        before_ref[...] = jnp.zeros_like(before_ref)
        low_ref[:slots, :] = jnp.zeros((slots, 128), jnp.float32)

    @pl.when(rank == 2 * CHIP_Z - 1)
    def _():
        after_ref[...] = jnp.zeros_like(after_ref)
        low_ref[2 * slots :, :] = jnp.zeros((slots, 128), jnp.float32)

    own = me.astype(jnp.float32)

    def along_z(position):
        level = level_of(position)
        whole(s, level, send_up.at[level], recv_z.at[level], at_c).wait_recv()
        spread(level)

    def diagonal(level):
        half_from_x(level).wait_recv()
        half_from_y(level).wait_recv()
        to_core(sd, level).start()

    middle = (has_above & has_below).astype(jnp.int32)

    def step_of(t):
        j, k = (t + 3) // 4 - 1, (t + 3) % 4
        column = (k == 0) & (j < CHIP_Z - 1) | (t == 0)
        slanted = (k == 3) & (j >= 1) | (t == 4 * CHIP_Z + 1)
        position = jnp.where(t == 0, 0, jnp.where(column, j + 1, jnp.where(slanted, j - 1, j)))
        seg = jnp.where(column, s, jnp.where(slanted, sd, jnp.where(k == 1, sx, sy)))
        return column | slanted | (k == 1) | (k == 2), seg * CHIP_Z + level_of(position)

    @pl.loop(0, 4 * CHIP_Z + 2)
    def _(t):
        j, k = (t + 3) // 4 - 1, (t + 3) % 4

        @pl.when((k == 0) & (j >= 0) & (j < CHIP_Z))
        def _():
            pl.when((middle == 1) & (j == 0))(lambda: along_z(1))
            pl.when(j + 1 + middle < CHIP_Z)(lambda: along_z(j + 1 + middle))
            level = level_of(j)
            from_x(level).wait_recv()
            half_to_y(level).start()
            to_core(sx, level).start()
            from_y(level).wait_recv()
            half_to_x(level).start()
            to_core(sy, level).start()

        pl.when((k == 2) & (j >= 1) & (j < CHIP_Z))(lambda: diagonal(level_of(j - 1)))
        pl.when(t == 4 * CHIP_Z + 1)(lambda: diagonal(level_of(CHIP_Z - 1)))
        active, chip = step_of(t)

        @pl.when(active)
        def _():
            from_core(chip).wait_recv()
            gathered, octants = [], []
            for c in range(2):
                block = held_ref[chip * 2 + c]
                mask = jnp.where(block[OWNERS:, :] == own, 1.0, 0.0)
                held, octant = chosen_children(block[:OWNERS, :], keys_of(mask, table_ref[EARLIER : EARLIER + 256, :256]), WIDTH // 2)
                gathered.append(held)
                octants.append(octant)
            mass, face = masses(
                jnp.concatenate(gathered, axis=1), jnp.concatenate(octants, axis=1), table_ref
            )
            lanes = pl.ds(pl.multiple_of(chip * WIDTH, WIDTH), WIDTH)
            mass_ref[:, lanes] = mass
            face_ref[:, lanes] = face
            low_ref[pl.ds(pl.multiple_of(slots + chip * WIDTH, WIDTH), WIDTH), :] = face[:128].T
            pl.when(t >= DELAY)(lambda: send_faces(chip))

        waiting, old = step_of(jnp.maximum(t - DELAY, 0))
        pl.when((t >= DELAY) & (t < 2 * DELAY) & waiting)(lambda: send_faces(old))

    @pl.loop(0, CHIP_Z)
    def _(level):
        pl.when(has_above & (level <= z))(lambda: up(level).wait_send())
        pl.when(has_below & (level >= z))(lambda: down(level).wait_send())
        to_x(level).wait_send()
        to_y(level).wait_send()
        half_to_x(level).wait_send()
        half_to_y(level).wait_send()

    @pl.loop(0, 4 * CHIP_Z)
    def _(chip):
        to_core(chip // CHIP_Z, chip % CHIP_Z).wait_send()

        @pl.when(has_next)
        def _():
            for copy in to_next(chip):
                copy.wait_send()
            for copy in from_next(chip):
                copy.wait_recv()

        @pl.when(has_prev)
        def _():
            for copy in to_prev(chip):
                copy.wait_send()
            for copy in from_prev(chip):
                copy.wait_recv()


def gather_and_compute(nodes, marks, owners, tables, cap):
    devices = 8 * CHIP_Z
    slots = devices * cap
    vmem = pl.BlockSpec(memory_space=pltpu.VMEM)
    faces = jax.ShapeDtypeStruct((FACES, slots), jnp.float32)
    low = jax.ShapeDtypeStruct((3 * slots, 128), jnp.float32)
    strips = jax.ShapeDtypeStruct((STRIP, slots), jnp.float32)
    dma = pltpu.SemaphoreType.DMA
    chips = 4 * CHIP_Z
    return pl.pallas_call(
        gather_kernel,
        in_specs=[vmem] * 4,
        out_specs=[vmem] * 5,
        out_shape=[jax.ShapeDtypeStruct((125, slots), jnp.float32), faces, low, strips, strips],
        scratch_shapes=[pltpu.VMEM((devices, OWNERS + 8, owners.shape[1]), jnp.float32)]
        + [dma((CHIP_Z,))] * 6
        + [dma((chips,))] * 5
        + [dma((CHIP_Z,))] * 5
        + [dma((chips,))] * 5,
        compiler_params=pltpu.CompilerParams(
            collective_id=0, has_side_effects=True, vmem_limit_bytes=48 * 1024 * 1024
        ),
        name="gather_and_compute",
    )(nodes, marks, owners, tables)


def assemble_kernel(link_ref, low_ref, before_ref, own_ref, after_ref, out_ref, high_ref, row_low, row_high):
    slots = own_ref.shape[1]
    for part, ref in enumerate((before_ref, own_ref, after_ref)):

        @pl.loop(0, slots // 512)
        def _(number):
            for k in range(4):
                start = pl.multiple_of(number * 512 + k * 128, 128)
                rows = pl.ds(pl.multiple_of(part * slots + number * 512 + k * 128, 128), 128)
                high_ref[rows, :STRIP] = ref[ref.shape[0] - STRIP :, pl.ds(start, 128)].T

    lane = lax.broadcasted_iota(jnp.int32, (1, 128), 1)
    under = [lane < 25 * (g + 1) for g in range(4)]

    @pl.loop(0, slots // 256)
    def _(number):
        for b in range(2):
            start = pl.multiple_of(number * 256 + b * 128, 128)
            for k in range(128):
                row = [link_ref[start + (f * slots + k)] for f in range(6)]
                value = low_ref[pl.ds(row[5], 1), :]
                for g in (3, 2, 1, 0):
                    value = jnp.where(under[g], low_ref[pl.ds(row[g ^ 1], 1), :], value)
                row_low[b, k : k + 1, :] = value
                row_high[b, k : k + 1, :] = high_ref[pl.ds(row[4], 1), :]

            low = row_low[b].T
            high = row_high[b, :, :STRIP].T
            fetched = [low[25 * (f ^ 1) : 25 * (f ^ 1) + 25] for f in range(4)]
            fetched += [high[0:25], low[100:125]]
            lanes = pl.ds(start, 128)
            own = [own_ref[0:125, lanes], own_ref[128:153, lanes]]
            out_ref[:, lanes] = jnp.concatenate(own, axis=0) + jnp.concatenate(fetched, axis=0)


def assemble(link, low, before, own, after):
    slots = own.shape[1]
    vmem = pl.BlockSpec(memory_space=pltpu.VMEM)
    return pl.pallas_call(
        assemble_kernel,
        in_specs=[pl.BlockSpec(memory_space=pltpu.SMEM), vmem, vmem, vmem, vmem],
        out_specs=vmem,
        out_shape=jax.ShapeDtypeStruct((150, slots), jnp.float32),
        scratch_shapes=[
            pltpu.VMEM((3 * slots, 128), jnp.float32),
            pltpu.VMEM((2, 128, 128), jnp.float32),
            pltpu.VMEM((2, 128, 128), jnp.float32),
        ],
        compiler_params=pltpu.CompilerParams(vmem_limit_bytes=48 * 1024 * 1024),
        name="assemble",
    )(link, low, before, own, after)


def body(parent_nodes, marks, child_owner, face_link):
    pick, tables = operators()
    devices = lax.axis_size("seg") * lax.axis_size("rank")
    me = lax.axis_index("seg") * lax.axis_size("rank") + lax.axis_index("rank")
    kids = child_owner.shape[0]
    cap = max(2, 2 * kids // devices)
    owners = child_owner.reshape(kids // 8, 8).T.astype(jnp.float32)
    if lax.axis_size("seg") == 4 and lax.axis_size("rank") == 2 * CHIP_Z and 2 * cap == WIDTH:
        mass, faces, low, before, after = gather_and_compute(parent_nodes.T, marks, owners, tables, cap)
    else:
        coords = lax.dot_general(
            jnp.asarray(pick, jnp.float32),
            parent_nodes[marks[0]],
            NT,
            precision=lax.Precision.HIGHEST,
            preferred_element_type=jnp.float32,
        )
        blocks = lax.all_gather(jnp.concatenate([coords, owners], axis=0), ("seg", "rank"))
        mask = (blocks[:, OWNERS:, :] == me.astype(jnp.float32)).astype(jnp.float32)
        mass, faces = geometry(blocks, mask, tables, cap)
        before = shifted(faces, "rank", 1)
        after = shifted(faces, "rank", -1)
        low = jnp.concatenate([before[:128].T, faces[:128].T, after[:128].T], axis=0)
        before, after = before[128:], after[128:]
    return (mass, assemble(face_link.T.reshape(-1), low, before, faces, after))


def solution(mesh):
    return jax.shard_map(
        body,
        mesh=mesh,
        in_specs=(
            P(("seg", "rank"), None),
            P(("seg", "rank"), None),
            P(("seg", "rank"), None),
            P(("seg", "rank"), None),
        ),
        out_specs=(P(None, ("seg", "rank")), P(None, ("seg", "rank"))),
        check_vma=False,
    )
```
